32 devices in a mesh: role: 4 (over y, x), atoms: 8 (over z, core).
Axes of the slice: x: 2, y: 2, z: 4, core: 2. Of those that a mesh axis runs over, the one named last changes fastest.
Arguments:
- features: bfloat16 [4, 8, 256, 256], P('role', 'atoms'), may hold values from -6 to 6
- positions: float32 [4, 8, 3, 256], P('role', 'atoms'), may hold values from 0 to 1, as said below
- neighbours: int32 [4, 8, 32, 256], P('role', 'atoms'), may hold values from 0 to 2304, as said below
- images: int32 [4, 8, 32, 256], P('role', 'atoms'), may hold values from 0 to 26
- wave: int32 [3, 2048], replicated, may hold values from -8 to 8, as said below
- kgain: float32 [256], replicated, may hold values from 0.5 to 4
- w_in: bfloat16 [256, 256], replicated, may hold values from -0.375 to 0.375
- w_query: bfloat16 [256, 256], replicated, may hold values from -0.375 to 0.375
- w_rbf: bfloat16 [64, 256], replicated, may hold values from -1.5 to 1.5
- b_rbf: float32 [256], replicated, may hold values from -4 to 4
- w_filter: bfloat16 [256, 256], replicated, may hold values from -0.375 to 0.375
- w_out: bfloat16 [256, 256], replicated, may hold values from -0.375 to 0.375
Outputs:
- updated: bfloat16 [4, 8, 256, 256], P('role', 'atoms')
The draws below stay inside these ranges and needn't reach their ends.
Inputs may be any that keep to these rules, and one draw needn't show every extreme that they name: `neighbours`: an entry (p * 3 + q) * 256 + t names atom t of the brick offset by p - 1 along the first and q - 1 along the second brick dimension, periodically; 2304 marks an empty slot. Empty slots come last; every list has 16 or more entries, and every brick has a full list. `positions`: atom coordinates of brick (a, b) lie in [a / 4, (a + 1) / 4) x [b / 8, (b + 1) / 8) x [0, 1). No wave vector has all three indices zero.
All inputs are finite; a program needn't handle non-finite values.
Results may differ from the reference program's by a relative error of at most 0.0085.
Values may be sent and summed in bfloat16 or wider, within the bound.
A program may use at most 128 MiB of HBM per device.

```python
import math
import jax
import jax.numpy as jnp
from jax import lax

F = 256
KV = 2048
RBF = 64
NBR = 32
ATOMS_DEV = 256
BRX = 4
BRY = 8


def draw_positions(key, part):
    spread = jax.random.uniform(key, (BRX, BRY, 3, ATOMS_DEV), jnp.float32)
    first_cell = jnp.arange(BRX, dtype=jnp.float32)[:, None, None]
    second_cell = jnp.arange(BRY, dtype=jnp.float32)[None, :, None]
    first_coord = (first_cell + spread[:, :, 0]) / BRX
    second_coord = (second_cell + spread[:, :, 1]) / BRY
    third_coord = spread[:, :, 2]
    return jnp.stack([first_coord, second_coord, third_coord], axis=2).astype(jnp.float32)


def draw_neighbours(key, part):
    key_picks = jax.random.fold_in(key, 11)
    key_fill = jax.random.fold_in(key, 12)
    picks = jax.random.randint(key_picks, (BRX, BRY, NBR, ATOMS_DEV), 0, 9 * ATOMS_DEV)
    filled = jax.random.randint(key_fill, (BRX, BRY, 1, ATOMS_DEV), NBR // 2, NBR + 1)
    atom_index = jnp.arange(ATOMS_DEV, dtype=jnp.int32)[None, None, None, :]
    filled = jnp.where(atom_index == 0, NBR, filled)
    slot_index = jnp.arange(NBR, dtype=jnp.int32)[None, None, :, None]
    return jnp.where(slot_index < filled, picks, 9 * ATOMS_DEV).astype(jnp.int32)


def draw_wave(key, part):
    indices = jax.random.randint(key, (3, KV), -8, 9)
    all_zero = jnp.all(indices == 0, axis=0)
    first_row = jnp.where(all_zero, 1, indices[0])
    return jnp.concatenate([first_row[None, :], indices[1:]], axis=0).astype(jnp.int32)


def with_ends(values, rng, low, top_value):
    longest = values.shape.index(max(values.shape))
    spots = []
    for shift in (0, 1):
        where = [jax.random.randint(jax.random.fold_in(rng, axis), (), 0, length) for axis, length in enumerate(values.shape)]
        where[longest] = (where[longest] + shift) % values.shape[longest]
        spots.append(tuple(where))
    return values.at[spots[0]].set(low).at[spots[1]].set(top_value)


def block_levels(own_key, extent, cuts, low, high):
    loudness, own = 1.0, jax.random.fold_in(own_key, 6)
    for dim, parts in cuts:
        heights = jnp.exp(jax.random.uniform(jax.random.fold_in(own, dim), (parts,), jnp.float32, low / len(cuts), high / len(cuts)))
        loudness = loudness * jnp.repeat(heights, extent[dim] // parts).reshape([-1 if axis == dim else 1 for axis in range(len(extent))])
    return loudness


def centred(rng, shape, scale, reach, split=(), kind=jnp.bfloat16):
    array = jax.random.normal(rng, shape, jnp.float32) * scale
    if len(split) > 0:
        array = block_levels(rng, shape, split, -0.22, 0.18) * array
    return jnp.clip(array, min=-reach, max=reach).astype(kind)


def setup_inputs(seed: int = 0) -> dict:
    key_list = jax.random.split(jax.random.key(seed), 13)
    features = centred(key_list[0], (BRX, BRY, ATOMS_DEV, F), 1.0, 6.0, ((0, 4), (1, 8)))
    positions = draw_positions(jax.random.fold_in(key_list[12], 71), 0)
    neighbours = draw_neighbours(jax.random.fold_in(key_list[12], 71), 0)
    images = with_ends(jax.random.randint(key_list[3], (BRX, BRY, NBR, ATOMS_DEV), 0, 27), jax.random.fold_in(key_list[3], 1), 0, 26).astype(jnp.int32)
    wave = draw_wave(jax.random.fold_in(key_list[12], 71), 0)
    kgain = jnp.clip(jnp.exp(jax.random.uniform(key_list[5], (F,), jnp.float32, math.log(0.5), math.log(4.0))), 0.5, 4.0)
    w_in = centred(key_list[6], (F, F), F ** -0.5, 0.375)
    w_query = centred(key_list[7], (F, F), F ** -0.5, 0.375)
    w_rbf = centred(key_list[8], (RBF, F), (RBF // 4) ** -0.5, 1.5)
    b_rbf = centred(key_list[9], (F,), 1.0, 4.0, (), jnp.float32)
    w_filter = centred(key_list[10], (F, F), F ** -0.5, 0.375)
    w_out = centred(key_list[11], (F, F), F ** -0.5, 0.375)
    return dict(features=features, positions=positions, neighbours=neighbours, images=images, wave=wave, kgain=kgain, w_in=w_in, w_query=w_query, w_rbf=w_rbf, b_rbf=b_rbf, w_filter=w_filter, w_out=w_out)


box_side = 1.0
soft_sq = 0.01
damping = 64.0
ewald_scale = 0.25

def shifted_softplus(values):
    return jax.nn.softplus(values) - math.log(2.0)

def pair_messages(near_table, near_coords, own_pos, near_slots, near_images, w_rbf, b_rbf, w_filter):
    slot_count, atom_count = near_slots.shape
    flat_slots = near_slots.reshape(-1)
    near_pos = near_coords[:, flat_slots].reshape(3, slot_count, atom_count)
    offsets = jnp.stack([near_images // 9 - 1, near_images // 3 % 3 - 1, near_images % 3 - 1]).astype(jnp.float32) * box_side
    delta = near_pos + offsets - own_pos[:, None, :]
    distance = jnp.sqrt(lax.optimization_barrier(jnp.sum(delta * delta, axis=0)) + soft_sq)
    basis_count = w_rbf.shape[0]
    centers = jnp.arange(basis_count, dtype=jnp.float32) * (4.0 / (basis_count - 1))
    sharpness = (basis_count / 4.0) ** 2
    basis = jnp.exp(-sharpness * (distance.reshape(-1, 1) - centers[None, :]) ** 2).astype(jnp.bfloat16)
    inner = shifted_softplus(jnp.dot(basis, w_rbf, preferred_element_type=jnp.float32) + b_rbf).astype(jnp.bfloat16)
    filters = jnp.dot(inner, w_filter, preferred_element_type=jnp.float32)
    gathered = near_table[flat_slots].astype(jnp.float32)
    return (filters * gathered).reshape(slot_count, atom_count, -1).sum(axis=0)

def phase_tables(own_pos, wave):
    vectors = wave.astype(jnp.float32) * (2.0 * math.pi / box_side)
    angle = lax.dot_general(own_pos, vectors, (((0,), (0,)), ((), ())), precision=lax.Precision.HIGHEST)
    return (jnp.cos(angle).astype(jnp.bfloat16), jnp.sin(angle).astype(jnp.bfloat16))

def wave_filter(wave, kgain):
    squares = lax.optimization_barrier(jnp.sum(wave.astype(jnp.float32) ** 2, axis=0))
    return ewald_scale * kgain[None, :] * (jnp.exp(-squares / damping) / squares)[:, None]

def contract_rows(left_side, right_side):
    return lax.dot_general(left_side, right_side, (((0,), (0,)), ((), ())), preferred_element_type=jnp.float32)

def reference(features, positions, neighbours, images, wave, kgain, w_in, w_query, w_rbf, b_rbf, w_filter, w_out):
    brick_total = BRX * BRY
    feat_width = features.shape[3]
    atom_total = brick_total * ATOMS_DEV
    hidden_x = jnp.dot(features.reshape(-1, feat_width), w_in, preferred_element_type=jnp.float32).astype(jnp.bfloat16)
    hidden_x = hidden_x.reshape(BRX, BRY, ATOMS_DEV, feat_width)
    k_filter = wave_filter(wave, kgain)
    brick_ids = jnp.arange(brick_total, dtype=jnp.int32)

    def accumulate(running, brick):
        brick_x = brick // BRY
        brick_y = brick % BRY
        own_rows = features[brick_x, brick_y]
        queries = jnp.dot(own_rows, w_query, preferred_element_type=jnp.float32).astype(jnp.bfloat16)
        cosine, sine = phase_tables(positions[brick_x, brick_y], wave)
        partial_value = jnp.stack([contract_rows(cosine, queries), contract_rows(sine, queries)])
        return (running + partial_value * atom_total ** (-0.5), None)
    totals, _ = lax.scan(accumulate, jnp.zeros((2, KV, feat_width), jnp.float32), brick_ids)
    filtered = (totals * k_filter[None]).astype(jnp.bfloat16)

    def one_brick(brick):
        brick_x = brick // BRY
        brick_y = brick % BRY
        table_parts = []
        coord_parts = []
        for step_x in range(3):
            for step_y in range(3):
                other_x = (brick_x + step_x - 1) % BRX
                other_y = (brick_y + step_y - 1) % BRY
                table_parts.append(hidden_x[other_x, other_y])
                coord_parts.append(positions[other_x, other_y])
        table_parts.append(jnp.zeros((1, feat_width), jnp.bfloat16))
        coord_parts.append(jnp.zeros((3, 1), jnp.float32))
        near_table = jnp.concatenate(table_parts, axis=0)
        near_coords = jnp.concatenate(coord_parts, axis=1)
        own_pos = positions[brick_x, brick_y]
        short_msg = pair_messages(near_table, near_coords, own_pos, neighbours[brick_x, brick_y], images[brick_x, brick_y], w_rbf, b_rbf, w_filter)
        cosine, sine = phase_tables(own_pos, wave)
        ewald = jnp.dot(cosine, filtered[0], preferred_element_type=jnp.float32) + jnp.dot(sine, filtered[1], preferred_element_type=jnp.float32)
        combined = (short_msg * NBR ** (-0.5) + ewald).astype(jnp.bfloat16)
        own_rows = features[brick_x, brick_y]
        return (own_rows.astype(jnp.float32) + jnp.dot(combined, w_out, preferred_element_type=jnp.float32)).astype(jnp.bfloat16)
    result = lax.map(one_brick, brick_ids)
    return result.reshape(BRX, BRY, ATOMS_DEV, feat_width)
```

```python
import functools
import math

import jax
import jax.numpy as jnp
from jax import lax
from jax.experimental import pallas as pl
from jax.experimental.pallas import tpu as pltpu
from jax.sharding import PartitionSpec as P

soft_sq = 0.01
damping = 64.0
ewald_scale = 0.25
coord_rows = 16
piece_rows = 16
MESH = pl.DeviceIdType.MESH


def contract_first(left, right):
    return lax.dot_general(
        left, right, (((0,), (0,)), ((), ())), preferred_element_type=jnp.float32
    )


def dot(left, right):
    return jnp.dot(left, right, preferred_element_type=jnp.float32)


def flipped(array):
    return jnp.transpose(array.astype(jnp.float32))


def turns_cos_sin(turns):
    r = turns - jnp.floor(turns + 0.5)
    u = r * r
    sin_half = jnp.full_like(u, -(math.pi**11) / math.factorial(11))
    for power in (9, 7, 5, 3, 1):
        sign = 1.0 if power % 4 == 1 else -1.0
        sin_half = sin_half * u + sign * math.pi**power / math.factorial(power)
    sin_half = sin_half * r
    cos_half = jnp.full_like(u, math.pi**12 / math.factorial(12))
    for power in (10, 8, 6, 4, 2, 0):
        sign = 1.0 if power % 4 == 0 else -1.0
        cos_half = cos_half * u + sign * math.pi**power / math.factorial(power)
    return 1.0 - 2.0 * sin_half * sin_half, 2.0 * sin_half * cos_half


def exchange_plan(role_count, atoms_count, rows):
    role, atoms = lax.axis_index("role"), lax.axis_index("atoms")
    core = atoms % 2
    role_bits = role_count.bit_length() - 1
    atom_bits = atoms_count.bit_length() - 1
    partners = [(core, (role, atoms + 1 - 2 * core))]
    for stage in range(role_bits):
        if role_bits == 2:
            which = (stage + core) % 2
            low, high = role % 2, (role // 2) % 2
            bit = low + which * (high - low)
            partners.append((bit, (role + (1 - 2 * bit) * (1 + which), atoms)))
        else:
            bit = (role // 2**stage) % 2
            partners.append((bit, (role + (1 - 2 * bit) * 2**stage, atoms)))
    for stage in range(1, atom_bits):
        bit = (atoms // 2**stage) % 2
        partners.append((bit, (role, atoms + (1 - 2 * bit) * 2**stage)))
    plan = []
    start, length = 0, rows
    for bit, device in partners:
        length //= 2
        keep = start + bit * length
        send = start + (1 - bit) * length
        plan.append((device, keep, send, length))
        start = keep
    return plan


def block_kernel(
    role_count,
    atoms_count,
    features,
    positions,
    neighbours,
    images,
    waves,
    kgain,
    w_in,
    w_query,
    w_rbf,
    b_rbf,
    w_filter,
    w_out,
    result,
    table,
    pieces,
    phase,
    phase_t,
    sums,
    staged,
    landed,
    filtered,
    gain,
    offsets,
    blocks,
    wide_a,
    wide_b,
    messages,
    rbf_t,
    filter_t,
    bias,
    halo_send,
    halo_recv,
    cut_send,
    cut_recv,
    join_send,
    join_recv,
):
    role, atoms = lax.axis_index("role"), lax.axis_index("atoms")
    atom_count, width = features.shape
    slot_count = neighbours.shape[0]
    wave_count = waves.shape[0]
    basis_count = w_rbf.shape[0]
    rows = 2 * wave_count
    plan = exchange_plan(role_count, atoms_count, rows)
    around = []
    for da in (-1, 0, 1):
        for db in (-1, 0, 1):
            if da or db:
                device = (
                    (role + da + role_count) % role_count,
                    (atoms + db + atoms_count) % atoms_count,
                )
                around.append((device, (1 - da) * 3 + (1 - db)))

    barrier = pltpu.get_barrier_semaphore()
    for device, _ in around:
        pl.semaphore_signal(barrier, inc=1, device_id=device, device_id_type=MESH)
    for device, _, _, _ in plan:
        pl.semaphore_signal(barrier, inc=1, device_id=device, device_id_type=MESH)

    own = positions[...]
    high = own.astype(jnp.bfloat16).astype(jnp.float32)
    rest = own - high
    middle = rest.astype(jnp.bfloat16).astype(jnp.float32)
    pieces[...] = jnp.zeros_like(pieces)
    pieces[0:3, :] = high
    pieces[3:6, :] = middle
    pieces[6:9, :] = rest - middle
    pos_pieces = pieces[...].astype(jnp.bfloat16)
    hidden = dot(features[...], w_in[...]).astype(jnp.bfloat16)
    table[4, 0:width, :] = flipped(hidden).astype(jnp.bfloat16)
    table[4, width : width + coord_rows, :] = pos_pieces

    pl.semaphore_wait(barrier, len(around) + len(plan))
    halo = []
    for number, (device, slot) in enumerate(around):
        copy = pltpu.make_async_remote_copy(
            src_ref=table.at[4],
            dst_ref=table.at[slot],
            send_sem=halo_send.at[number],
            recv_sem=halo_recv.at[number],
            device_id=device,
            device_id_type=MESH,
        )
        copy.start()
        halo.append(copy)

    queries = dot(features[...], w_query[...]).astype(jnp.bfloat16)
    chunk = 256

    @pl.loop(0, wave_count // chunk)
    def _(step):
        first = pl.multiple_of(step * chunk, chunk)
        turns = dot(waves[pl.ds(first, chunk), :], pos_pieces)
        cosine, sine = turns_cos_sin(turns)
        cosine, sine = cosine.astype(jnp.bfloat16), sine.astype(jnp.bfloat16)
        phase[pl.ds(first, chunk), :] = cosine
        phase[pl.ds(wave_count + first, chunk), :] = sine
        sums[pl.ds(first, chunk), :] = dot(cosine, queries)
        sums[pl.ds(wave_count + first, chunk), :] = dot(sine, queries)

    def cut(stage):
        device, _, send, length = plan[stage]
        place = rows - 2 * length
        staged[pl.ds(place, length), :] = sums[
            pl.ds(pl.multiple_of(send, piece_rows), length), :
        ].astype(jnp.bfloat16)
        copy = pltpu.make_async_remote_copy(
            src_ref=staged.at[pl.ds(place, length)],
            dst_ref=landed.at[pl.ds(place, length)],
            send_sem=cut_send.at[stage],
            recv_sem=cut_recv.at[stage],
            device_id=device,
            device_id_type=MESH,
        )
        copy.start()
        return copy

    def add_cut(stage):
        _, keep, _, length = plan[stage]
        place = rows - 2 * length
        where = pl.ds(pl.multiple_of(keep, piece_rows), length)
        sums[where, :] = sums[where, :] + landed[pl.ds(place, length), :].astype(jnp.float32)

    def join(stage):
        device, keep, _, length = plan[stage]
        where = pl.ds(pl.multiple_of(keep, piece_rows), length)
        copy = pltpu.make_async_remote_copy(
            src_ref=filtered.at[where],
            dst_ref=filtered.at[where],
            send_sem=join_send.at[stage],
            recv_sem=join_recv.at[stage],
            device_id=device,
            device_id_type=MESH,
        )
        copy.start()
        return copy

    in_flight = cut(0)

    rbf_t[...] = flipped(w_rbf[...]).astype(jnp.bfloat16)
    filter_t[...] = flipped(w_filter[...]).astype(jnp.bfloat16)
    bias[...] = jnp.transpose(jnp.broadcast_to(b_rbf[...], (atom_count, width)))
    entry = neighbours[...]
    brick = entry // atom_count
    blocks[0] = brick.astype(jnp.float32)
    blocks[1] = (entry - brick * atom_count).astype(jnp.float32)
    image = images[...]
    first_part = jnp.where(image >= 9, 1, 0) + jnp.where(image >= 18, 1, 0)
    left = image - 9 * first_part
    second_part = jnp.where(left >= 3, 1, 0) + jnp.where(left >= 6, 1, 0)
    third_part = left - 3 * second_part
    for axis, part in enumerate((first_part, second_part, third_part)):
        offsets[axis] = (part - 1).astype(jnp.float32) - own[axis : axis + 1, :]
    messages[...] = jnp.zeros_like(messages)

    wave_part = waves[...]
    picks = jnp.where(
        lax.broadcasted_iota(jnp.int32, (waves.shape[1], 128), 0) < 3, 1.0, 0.0
    ).astype(jnp.bfloat16)
    squares = dot(wave_part * wave_part, picks)
    gain[...] = jnp.exp(squares * (-1.0 / damping)) / squares

    @pl.loop(0, rows // chunk)
    def _(step):
        first = pl.multiple_of(step * chunk, chunk)
        phase_t[:, pl.ds(first, chunk)] = flipped(phase[pl.ds(first, chunk), :]).astype(
            jnp.bfloat16
        )

    lane_atoms = lax.broadcasted_iota(jnp.int32, (atom_count, atom_count), 0).astype(
        jnp.float32
    ).astype(jnp.bfloat16)
    centers = lax.broadcasted_iota(jnp.int32, (basis_count, atom_count), 0).astype(
        jnp.float32
    ) * (4.0 / (basis_count - 1))
    sharpness = (basis_count / 4.0) ** 2
    one, zero = jnp.ones((), jnp.bfloat16), jnp.zeros((), jnp.bfloat16)

    def gather(slot, target):
        brick_row = blocks[0, pl.ds(slot, 1), :]
        atom_row = blocks[1, pl.ds(slot, 1), :]
        total = jnp.zeros((width + coord_rows, atom_count), jnp.float32)
        for number in range(9):
            wanted = jnp.where(brick_row == float(number), atom_row, -1.0).astype(jnp.bfloat16)
            chosen = jnp.where(lane_atoms == wanted, one, zero)
            total += dot(table[number], chosen)
        target[...] = total

    def filter_slot(slot, source):
        square = jnp.full((1, atom_count), soft_sq, jnp.float32)
        for axis in range(3):
            near = (
                source[width + axis : width + axis + 1, :]
                + source[width + 3 + axis : width + 4 + axis, :]
                + source[width + 6 + axis : width + 7 + axis, :]
            )
            delta = near + offsets[axis, pl.ds(slot, 1), :]
            square += delta * delta
        away = jnp.sqrt(square) - centers
        basis = jnp.exp(-sharpness * (away * away)).astype(jnp.bfloat16)
        before = dot(rbf_t[...], basis) + bias[...]
        inner = (
            jnp.maximum(before, 0.0)
            + jnp.log(1.0 + jnp.exp(-jnp.abs(before)))
            - math.log(2.0)
        ).astype(jnp.bfloat16)
        messages[...] += dot(filter_t[...], inner) * source[0:width, :]

    pairs = slot_count // 2

    def short_range(first, last):
        if last <= first:
            return

        @pl.loop(first, last)
        def _(pair):
            slot = pair * 2
            gather(slot + 1, wide_b)
            filter_slot(slot, wide_a)
            gather(lax.rem(slot + 2, slot_count), wide_a)
            filter_slot(slot + 1, wide_b)

    for copy in halo:
        copy.wait()
    gather(0, wide_a)

    stages = len(plan)
    share = [pairs * step // (2 * stages - 1) for step in range(2 * stages)]
    for stage in range(stages):
        if stage:
            short_range(share[stage - 1], share[stage])
        in_flight.wait()
        add_cut(stage)
        if stage + 1 < stages:
            in_flight = cut(stage + 1)

    _, mine, _, mine_rows = plan[-1]
    scale = (atom_count * role_count * atoms_count) ** (-0.5) * ewald_scale
    channel = kgain[...] * scale
    where = pl.ds(pl.multiple_of(mine, piece_rows), mine_rows)
    gain_rows = gain[pl.ds(pl.multiple_of(mine % wave_count, piece_rows), mine_rows), :]
    for part in range(width // 128):
        lanes = pl.ds(part * 128, 128)
        filtered[where, lanes] = (
            sums[where, lanes] * gain_rows * channel[:, part * 128 : part * 128 + 128]
        ).astype(jnp.bfloat16)

    for number, stage in enumerate(reversed(range(stages))):
        in_flight = join(stage)
        short_range(share[stages - 1 + number], share[stages + number])
        if number == stages - 1:
            short = jnp.transpose(messages[...]) * slot_count ** (-0.5)
        in_flight.wait()

    combined = (short + dot(phase_t[...], filtered[...])).astype(jnp.bfloat16)
    result[...] = (features[...].astype(jnp.float32) + dot(combined, w_out[...])).astype(
        jnp.bfloat16
    )


def local(
    role_count,
    atoms_count,
    features,
    positions,
    neighbours,
    images,
    wave,
    kgain,
    w_in,
    w_query,
    w_rbf,
    b_rbf,
    w_filter,
    w_out,
):
    own_rows = features[0, 0]
    atom_count, width = own_rows.shape
    wave_count = wave.shape[1]
    slot_count = neighbours.shape[2]
    rows = 2 * wave_count
    stages = (role_count * atoms_count).bit_length() - 1
    waves = jnp.transpose(
        jnp.pad(jnp.concatenate([wave] * 3, axis=0), ((0, piece_rows - 9), (0, 0)))
    ).astype(jnp.bfloat16)
    vmem = pl.BlockSpec(memory_space=pltpu.VMEM)
    full = width + coord_rows
    out = pl.pallas_call(
        functools.partial(block_kernel, role_count, atoms_count),
        out_shape=jax.ShapeDtypeStruct((atom_count, width), jnp.bfloat16),
        in_specs=[vmem] * 12,
        out_specs=vmem,
        scratch_shapes=[
            pltpu.VMEM((9, full, atom_count), jnp.bfloat16),
            pltpu.VMEM((piece_rows, atom_count), jnp.float32),
            pltpu.VMEM((rows, atom_count), jnp.bfloat16),
            pltpu.VMEM((atom_count, rows), jnp.bfloat16),
            pltpu.VMEM((rows, width), jnp.float32),
            pltpu.VMEM((rows, width), jnp.bfloat16),
            pltpu.VMEM((rows, width), jnp.bfloat16),
            pltpu.VMEM((rows, width), jnp.bfloat16),
            pltpu.VMEM((wave_count, 128), jnp.float32),
            pltpu.VMEM((3, slot_count, atom_count), jnp.float32),
            pltpu.VMEM((2, slot_count, atom_count), jnp.float32),
            pltpu.VMEM((full, atom_count), jnp.float32),
            pltpu.VMEM((full, atom_count), jnp.float32),
            pltpu.VMEM((width, atom_count), jnp.float32),
            pltpu.VMEM((width, w_rbf.shape[0]), jnp.bfloat16),
            pltpu.VMEM((width, width), jnp.bfloat16),
            pltpu.VMEM((width, atom_count), jnp.float32),
            pltpu.SemaphoreType.DMA((8,)),
            pltpu.SemaphoreType.DMA((8,)),
            pltpu.SemaphoreType.DMA((stages,)),
            pltpu.SemaphoreType.DMA((stages,)),
            pltpu.SemaphoreType.DMA((stages,)),
            pltpu.SemaphoreType.DMA((stages,)),
        ],
        compiler_params=pltpu.CompilerParams(
            collective_id=0, has_side_effects=True, vmem_limit_bytes=48 * 1024 * 1024
        ),
    )(
        own_rows,
        positions[0, 0],
        neighbours[0, 0],
        images[0, 0],
        waves,
        kgain[None, :],
        w_in,
        w_query,
        w_rbf,
        b_rbf[None, :],
        w_filter,
        w_out,
    )
    return out[None, None]


def solution(mesh):
    placed = P("role", "atoms", None, None)
    body = functools.partial(local, mesh.shape["role"], mesh.shape["atoms"])
    return jax.shard_map(
        body,
        mesh=mesh,
        in_specs=(placed,) * 4 + (P(),) * 8,
        out_specs=placed,
        check_vma=False,
    )
```

```python
import functools
import math

import jax
import jax.numpy as jnp
from jax import lax
from jax.experimental import pallas as pl
from jax.experimental.pallas import tpu as pltpu
from jax.sharding import PartitionSpec as P

soft_sq = 0.01
damping = 64.0
ewald_scale = 0.25
coord_rows = 16
piece_rows = 16
MESH = pl.DeviceIdType.MESH


def contract_first(left, right):
    return lax.dot_general(
        left, right, (((0,), (0,)), ((), ())), preferred_element_type=jnp.float32
    )


def dot(left, right):
    return jnp.dot(left, right, preferred_element_type=jnp.float32)


def flipped(array):
    return jnp.transpose(array.astype(jnp.float32))


def turns_cos_sin(turns):
    r = turns - jnp.floor(turns + 0.5)
    u = r * r
    sin_half = jnp.full_like(u, -(math.pi**11) / math.factorial(11))
    for power in (9, 7, 5, 3, 1):
        sign = 1.0 if power % 4 == 1 else -1.0
        sin_half = sin_half * u + sign * math.pi**power / math.factorial(power)
    sin_half = sin_half * r
    cos_half = jnp.full_like(u, math.pi**12 / math.factorial(12))
    for power in (10, 8, 6, 4, 2, 0):
        sign = 1.0 if power % 4 == 0 else -1.0
        cos_half = cos_half * u + sign * math.pi**power / math.factorial(power)
    return 1.0 - 2.0 * sin_half * sin_half, 2.0 * sin_half * cos_half


def exchange_plan(role_count, atoms_count, rows):
    role, atoms = lax.axis_index("role"), lax.axis_index("atoms")
    core = atoms % 2
    role_bits = role_count.bit_length() - 1
    atom_bits = atoms_count.bit_length() - 1
    partners = [(core, (role, atoms + 1 - 2 * core))]
    for stage in range(role_bits):
        if role_bits == 2:
            which = (stage + core) % 2
            low, high = role % 2, (role // 2) % 2
            bit = low + which * (high - low)
            partners.append((bit, (role + (1 - 2 * bit) * (1 + which), atoms)))
        else:
            bit = (role // 2**stage) % 2
            partners.append((bit, (role + (1 - 2 * bit) * 2**stage, atoms)))
    for stage in range(1, atom_bits):
        bit = (atoms // 2**stage) % 2
        partners.append((bit, (role, atoms + (1 - 2 * bit) * 2**stage)))
    plan = []
    start, length = 0, rows
    for bit, device in partners:
        length //= 2
        keep = start + bit * length
        send = start + (1 - bit) * length
        plan.append((device, keep, send, length))
        start = keep
    return plan


def block_kernel(
    role_count,
    atoms_count,
    features,
    positions,
    neighbours,
    images,
    waves,
    kgain,
    w_in,
    w_query,
    w_rbf,
    b_rbf,
    w_filter,
    w_out,
    result,
    table,
    pieces,
    phase,
    phase_t,
    sums,
    staged,
    landed,
    filtered,
    gain,
    offsets,
    blocks,
    wide_a,
    wide_b,
    messages,
    rbf_t,
    filter_t,
    bias,
    halo_send,
    halo_recv,
    cut_send,
    cut_recv,
    join_send,
    join_recv,
):
    role, atoms = lax.axis_index("role"), lax.axis_index("atoms")
    atom_count, width = features.shape
    slot_count = neighbours.shape[0]
    wave_count = waves.shape[0]
    basis_count = w_rbf.shape[0]
    rows = 2 * wave_count
    plan = exchange_plan(role_count, atoms_count, rows)
    beside, along = [], []
    for step in (-1, 1):
        device = ((role + step + role_count) % role_count, atoms)
        beside.append((device, 1, 1 - step, 1))
        device = (role, (atoms + step + atoms_count) % atoms_count)
        along.extend((device, p, p, 1 - step) for p in (1, 0, 2))

    barrier = pltpu.get_barrier_semaphore()
    greeted = [beside[0][0], beside[1][0], along[0][0], along[3][0]]
    for device in greeted:
        pl.semaphore_signal(barrier, inc=1, device_id=device, device_id_type=MESH)
    for device, _, _, _ in plan:
        pl.semaphore_signal(barrier, inc=1, device_id=device, device_id_type=MESH)

    own = positions[...]
    high = own.astype(jnp.bfloat16).astype(jnp.float32)
    rest = own - high
    middle = rest.astype(jnp.bfloat16).astype(jnp.float32)
    pieces[...] = jnp.zeros_like(pieces)
    pieces[0:3, :] = high
    pieces[3:6, :] = middle
    pieces[6:9, :] = rest - middle
    pos_pieces = pieces[...].astype(jnp.bfloat16)
    hidden = dot(features[...], w_in[...]).astype(jnp.bfloat16)
    table[4, 0:width, :] = flipped(hidden).astype(jnp.bfloat16)
    table[4, width : width + coord_rows, :] = pos_pieces

    pl.semaphore_wait(barrier, len(greeted) + len(plan))

    def send_brick(number, device, p, to_p, to_q):
        copy = pltpu.make_async_remote_copy(
            src_ref=table.at[p * 3 + 1],
            dst_ref=table.at[to_p * 3 + to_q],
            send_sem=halo_send.at[number],
            recv_sem=halo_recv.at[number],
            device_id=device,
            device_id_type=MESH,
        )
        copy.start()
        return copy

    halo = [send_brick(number, *move) for number, move in enumerate(beside)]

    queries = dot(features[...], w_query[...]).astype(jnp.bfloat16)
    chunk = 256

    @pl.loop(0, wave_count // chunk)
    def _(step):
        first = pl.multiple_of(step * chunk, chunk)
        turns = dot(waves[pl.ds(first, chunk), :], pos_pieces)
        cosine, sine = turns_cos_sin(turns)
        cosine, sine = cosine.astype(jnp.bfloat16), sine.astype(jnp.bfloat16)
        phase[pl.ds(first, chunk), :] = cosine
        phase[pl.ds(wave_count + first, chunk), :] = sine
        sums[pl.ds(first, chunk), :] = dot(cosine, queries)
        sums[pl.ds(wave_count + first, chunk), :] = dot(sine, queries)

    def cut(stage):
        device, _, send, length = plan[stage]
        place = rows - 2 * length
        staged[pl.ds(place, length), :] = sums[
            pl.ds(pl.multiple_of(send, piece_rows), length), :
        ].astype(jnp.bfloat16)
        copy = pltpu.make_async_remote_copy(
            src_ref=staged.at[pl.ds(place, length)],
            dst_ref=landed.at[pl.ds(place, length)],
            send_sem=cut_send.at[stage],
            recv_sem=cut_recv.at[stage],
            device_id=device,
            device_id_type=MESH,
        )
        copy.start()
        return copy

    def add_cut(stage):
        _, keep, _, length = plan[stage]
        place = rows - 2 * length
        where = pl.ds(pl.multiple_of(keep, piece_rows), length)
        sums[where, :] = sums[where, :] + landed[pl.ds(place, length), :].astype(jnp.float32)

    def join(stage):
        device, keep, _, length = plan[stage]
        where = pl.ds(pl.multiple_of(keep, piece_rows), length)
        copy = pltpu.make_async_remote_copy(
            src_ref=filtered.at[where],
            dst_ref=filtered.at[where],
            send_sem=join_send.at[stage],
            recv_sem=join_recv.at[stage],
            device_id=device,
            device_id_type=MESH,
        )
        copy.start()
        return copy

    in_flight = cut(0)
    for copy in halo:
        copy.wait()
    halo = [send_brick(2 + number, *move) for number, move in enumerate(along)]

    rbf_t[...] = flipped(w_rbf[...]).astype(jnp.bfloat16)
    filter_t[...] = flipped(w_filter[...]).astype(jnp.bfloat16)
    bias[...] = jnp.transpose(jnp.broadcast_to(b_rbf[...], (atom_count, width)))
    entry = neighbours[...]
    brick = entry // atom_count
    blocks[0] = brick.astype(jnp.float32)
    blocks[1] = (entry - brick * atom_count).astype(jnp.float32)
    image = images[...]
    first_part = jnp.where(image >= 9, 1, 0) + jnp.where(image >= 18, 1, 0)
    left = image - 9 * first_part
    second_part = jnp.where(left >= 3, 1, 0) + jnp.where(left >= 6, 1, 0)
    third_part = left - 3 * second_part
    for axis, part in enumerate((first_part, second_part, third_part)):
        offsets[axis] = (part - 1).astype(jnp.float32) - own[axis : axis + 1, :]
    messages[...] = jnp.zeros_like(messages)

    wave_part = waves[...]
    picks = jnp.where(
        lax.broadcasted_iota(jnp.int32, (waves.shape[1], 128), 0) < 3, 1.0, 0.0
    ).astype(jnp.bfloat16)
    squares = dot(wave_part * wave_part, picks)
    gain[...] = jnp.exp(squares * (-1.0 / damping)) / squares

    in_flight.wait()
    add_cut(0)
    in_flight = cut(1)

    @pl.loop(0, rows // chunk)
    def _(step):
        first = pl.multiple_of(step * chunk, chunk)
        phase_t[:, pl.ds(first, chunk)] = flipped(phase[pl.ds(first, chunk), :]).astype(
            jnp.bfloat16
        )

    lane_atoms = lax.broadcasted_iota(jnp.int32, (atom_count, atom_count), 0).astype(
        jnp.float32
    ).astype(jnp.bfloat16)
    centers = lax.broadcasted_iota(jnp.int32, (basis_count, atom_count), 0).astype(
        jnp.float32
    ) * (4.0 / (basis_count - 1))
    sharpness = (basis_count / 4.0) ** 2
    one, zero = jnp.ones((), jnp.bfloat16), jnp.zeros((), jnp.bfloat16)

    def gather(slot, target):
        brick_row = blocks[0, pl.ds(slot, 1), :]
        atom_row = blocks[1, pl.ds(slot, 1), :]
        chosen = []
        for number in range(9):
            wanted = jnp.where(brick_row == float(number), atom_row, -1.0).astype(jnp.bfloat16)
            chosen.append(jnp.where(lane_atoms == wanted, one, zero))
        bricks = jnp.concatenate([table[number] for number in range(9)], axis=1)
        target[...] = dot(bricks, jnp.concatenate(chosen, axis=0))

    def filter_slot(slot, source):
        square = jnp.full((1, atom_count), soft_sq, jnp.float32)
        for axis in range(3):
            near = (
                source[width + axis : width + axis + 1, :]
                + source[width + 3 + axis : width + 4 + axis, :]
                + source[width + 6 + axis : width + 7 + axis, :]
            )
            delta = near + offsets[axis, pl.ds(slot, 1), :]
            square += delta * delta
        away = jnp.sqrt(square) - centers
        basis = jnp.exp(-sharpness * (away * away)).astype(jnp.bfloat16)
        before = dot(rbf_t[...], basis) + bias[...]
        inner = (
            jnp.maximum(before, 0.0)
            + jnp.log(1.0 + jnp.exp(-jnp.abs(before)))
            - math.log(2.0)
        ).astype(jnp.bfloat16)
        messages[...] += dot(filter_t[...], inner) * source[0:width, :]

    pairs = slot_count // 2

    def short_range(first, last):
        if last <= first:
            return

        @pl.loop(first, last)
        def _(pair):
            slot = pair * 2
            gather(slot + 1, wide_b)
            filter_slot(slot, wide_a)
            gather(lax.rem(slot + 2, slot_count), wide_a)
            filter_slot(slot + 1, wide_b)

    stages = len(plan)
    windows = 2 * stages - 2
    share = [pairs * step // windows for step in range(windows + 1)]
    for stage in range(1, stages):
        if stage == 2:
            for copy in halo:
                copy.wait()
            gather(0, wide_a)
        if stage > 1:
            short_range(share[stage - 2], share[stage - 1])
        in_flight.wait()
        add_cut(stage)
        if stage + 1 < stages:
            in_flight = cut(stage + 1)

    _, mine, _, mine_rows = plan[-1]
    scale = (atom_count * role_count * atoms_count) ** (-0.5) * ewald_scale
    channel = kgain[...] * scale
    where = pl.ds(pl.multiple_of(mine, piece_rows), mine_rows)
    gain_rows = gain[pl.ds(pl.multiple_of(mine % wave_count, piece_rows), mine_rows), :]
    for part in range(width // 128):
        lanes = pl.ds(part * 128, 128)
        filtered[where, lanes] = (
            sums[where, lanes] * gain_rows * channel[:, part * 128 : part * 128 + 128]
        ).astype(jnp.bfloat16)

    for number, stage in enumerate(reversed(range(stages))):
        in_flight = join(stage)
        short_range(share[stages - 2 + number], share[stages - 1 + number])
        if number == stages - 1:
            short = jnp.transpose(messages[...]) * slot_count ** (-0.5)
        in_flight.wait()

    combined = (short + dot(phase_t[...], filtered[...])).astype(jnp.bfloat16)
    result[...] = (features[...].astype(jnp.float32) + dot(combined, w_out[...])).astype(
        jnp.bfloat16
    )


def local(
    role_count,
    atoms_count,
    features,
    positions,
    neighbours,
    images,
    wave,
    kgain,
    w_in,
    w_query,
    w_rbf,
    b_rbf,
    w_filter,
    w_out,
):
    own_rows = features[0, 0]
    atom_count, width = own_rows.shape
    wave_count = wave.shape[1]
    slot_count = neighbours.shape[2]
    rows = 2 * wave_count
    stages = (role_count * atoms_count).bit_length() - 1
    waves = jnp.transpose(
        jnp.pad(jnp.concatenate([wave] * 3, axis=0), ((0, piece_rows - 9), (0, 0)))
    ).astype(jnp.bfloat16)
    vmem = pl.BlockSpec(memory_space=pltpu.VMEM)
    full = width + coord_rows
    out = pl.pallas_call(
        functools.partial(block_kernel, role_count, atoms_count),
        out_shape=jax.ShapeDtypeStruct((atom_count, width), jnp.bfloat16),
        in_specs=[vmem] * 12,
        out_specs=vmem,
        scratch_shapes=[
            pltpu.VMEM((9, full, atom_count), jnp.bfloat16),
            pltpu.VMEM((piece_rows, atom_count), jnp.float32),
            pltpu.VMEM((rows, atom_count), jnp.bfloat16),
            pltpu.VMEM((atom_count, rows), jnp.bfloat16),
            pltpu.VMEM((rows, width), jnp.float32),
            pltpu.VMEM((rows, width), jnp.bfloat16),
            pltpu.VMEM((rows, width), jnp.bfloat16),
            pltpu.VMEM((rows, width), jnp.bfloat16),
            pltpu.VMEM((wave_count, 128), jnp.float32),
            pltpu.VMEM((3, slot_count, atom_count), jnp.float32),
            pltpu.VMEM((2, slot_count, atom_count), jnp.float32),
            pltpu.VMEM((full, atom_count), jnp.float32),
            pltpu.VMEM((full, atom_count), jnp.float32),
            pltpu.VMEM((width, atom_count), jnp.float32),
            pltpu.VMEM((width, w_rbf.shape[0]), jnp.bfloat16),
            pltpu.VMEM((width, width), jnp.bfloat16),
            pltpu.VMEM((width, atom_count), jnp.float32),
            pltpu.SemaphoreType.DMA((8,)),
            pltpu.SemaphoreType.DMA((8,)),
            pltpu.SemaphoreType.DMA((stages,)),
            pltpu.SemaphoreType.DMA((stages,)),
            pltpu.SemaphoreType.DMA((stages,)),
            pltpu.SemaphoreType.DMA((stages,)),
        ],
        compiler_params=pltpu.CompilerParams(
            collective_id=0, has_side_effects=True, vmem_limit_bytes=48 * 1024 * 1024
        ),
    )(
        own_rows,
        positions[0, 0],
        neighbours[0, 0],
        images[0, 0],
        waves,
        kgain[None, :],
        w_in,
        w_query,
        w_rbf,
        b_rbf[None, :],
        w_filter,
        w_out,
    )
    return out[None, None]


def solution(mesh):
    placed = P("role", "atoms", None, None)
    body = functools.partial(local, mesh.shape["role"], mesh.shape["atoms"])
    return jax.shard_map(
        body,
        mesh=mesh,
        in_specs=(placed,) * 4 + (P(),) * 8,
        out_specs=placed,
        check_vma=False,
    )
```

```python
import functools
import math

import jax
import jax.numpy as jnp
from jax import lax
from jax.experimental import pallas as pl
from jax.experimental.pallas import tpu as pltpu
from jax.sharding import PartitionSpec as P

soft_sq = 0.01
damping = 64.0
ewald_scale = 0.25
coord_rows = 16
piece_rows = 16
MESH = pl.DeviceIdType.MESH


def contract_first(left, right):
    return lax.dot_general(
        left, right, (((0,), (0,)), ((), ())), preferred_element_type=jnp.float32
    )


def dot(left, right):
    return jnp.dot(left, right, preferred_element_type=jnp.float32)


def flipped(array):
    return jnp.transpose(array.astype(jnp.float32))


def turns_cos_sin(turns):
    r = turns - jnp.floor(turns + 0.5)
    u = r * r
    sin_half = jnp.full_like(u, -(math.pi**11) / math.factorial(11))
    for power in (9, 7, 5, 3, 1):
        sign = 1.0 if power % 4 == 1 else -1.0
        sin_half = sin_half * u + sign * math.pi**power / math.factorial(power)
    sin_half = sin_half * r
    cos_half = jnp.full_like(u, math.pi**12 / math.factorial(12))
    for power in (10, 8, 6, 4, 2, 0):
        sign = 1.0 if power % 4 == 0 else -1.0
        cos_half = cos_half * u + sign * math.pi**power / math.factorial(power)
    return 1.0 - 2.0 * sin_half * sin_half, 2.0 * sin_half * cos_half


def exchange_plan(role_count, atoms_count, start, rows):
    role, atoms = lax.axis_index("role"), lax.axis_index("atoms")
    core = atoms % 2
    role_bits = role_count.bit_length() - 1
    atom_bits = atoms_count.bit_length() - 1
    partners = [(core, (role, atoms + 1 - 2 * core))]
    for stage in range(role_bits):
        if role_bits == 2:
            which = (stage + core) % 2
            low, high = role % 2, (role // 2) % 2
            bit = low + which * (high - low)
            partners.append((bit, (role + (1 - 2 * bit) * (1 + which), atoms)))
        else:
            bit = (role // 2**stage) % 2
            partners.append((bit, (role + (1 - 2 * bit) * 2**stage, atoms)))
    for stage in range(1, atom_bits):
        bit = (atoms // 2**stage) % 2
        partners.append((bit, (role, atoms + (1 - 2 * bit) * 2**stage)))
    plan = []
    length = rows
    for bit, device in partners:
        length //= 2
        keep = start + bit * length
        send = start + (1 - bit) * length
        plan.append((device, keep, send, length))
        start = keep
    return plan


def block_kernel(
    role_count,
    atoms_count,
    features,
    positions,
    neighbours,
    images,
    waves,
    kgain,
    w_in,
    w_query,
    w_rbf,
    b_rbf,
    w_filter,
    w_out,
    result,
    table,
    pieces,
    phase,
    phase_t,
    sums,
    staged,
    landed,
    filtered,
    gain,
    offsets,
    blocks,
    wide_a,
    wide_b,
    messages,
    rbf_t,
    filter_t,
    bias,
    halo_send,
    halo_recv,
    cut_send,
    cut_recv,
    join_send,
    join_recv,
):
    role, atoms = lax.axis_index("role"), lax.axis_index("atoms")
    atom_count, width = features.shape
    slot_count = neighbours.shape[0]
    wave_count = waves.shape[0]
    basis_count = w_rbf.shape[0]
    rows = 2 * wave_count
    chains = 2 if rows // (role_count * atoms_count) >= 2 * piece_rows else 1
    chain_rows = rows // chains
    chain_waves = wave_count // chains
    plans = [
        exchange_plan(role_count, atoms_count, chain * chain_rows, chain_rows)
        for chain in range(chains)
    ]
    plan = plans[0]
    stages = len(plan)
    beside, along = [], []
    for step in (-1, 1):
        device = ((role + step + role_count) % role_count, atoms)
        beside.append((device, 1, 1 - step, 1))
        device = (role, (atoms + step + atoms_count) % atoms_count)
        along.extend((device, p, p, 1 - step) for p in (1, 0, 2))

    barrier = pltpu.get_barrier_semaphore()
    greeted = [beside[0][0], beside[1][0], along[0][0], along[3][0]]
    for device in greeted:
        pl.semaphore_signal(barrier, inc=1, device_id=device, device_id_type=MESH)
    for device, _, _, _ in plan:
        pl.semaphore_signal(barrier, inc=1, device_id=device, device_id_type=MESH)

    own = positions[...]
    high = own.astype(jnp.bfloat16).astype(jnp.float32)
    rest = own - high
    middle = rest.astype(jnp.bfloat16).astype(jnp.float32)
    pieces[...] = jnp.zeros_like(pieces)
    pieces[0:3, :] = high
    pieces[3:6, :] = middle
    pieces[6:9, :] = rest - middle
    pos_pieces = pieces[...].astype(jnp.bfloat16)
    hidden = dot(features[...], w_in[...]).astype(jnp.bfloat16)
    table[4, 0:width, :] = flipped(hidden).astype(jnp.bfloat16)
    table[4, width : width + coord_rows, :] = pos_pieces

    pl.semaphore_wait(barrier, len(greeted) + len(plan))

    def send_brick(number, device, p, to_p, to_q):
        copy = pltpu.make_async_remote_copy(
            src_ref=table.at[p * 3 + 1],
            dst_ref=table.at[to_p * 3 + to_q],
            send_sem=halo_send.at[number],
            recv_sem=halo_recv.at[number],
            device_id=device,
            device_id_type=MESH,
        )
        copy.start()
        return copy

    halo = [send_brick(number, *move) for number, move in enumerate(beside)]

    queries = dot(features[...], w_query[...]).astype(jnp.bfloat16)
    chunk = 256

    def fill(chain):
        @pl.loop(0, chain_waves // chunk)
        def _(step):
            first = pl.multiple_of(step * chunk, chunk)
            turns = dot(waves[pl.ds(chain * chain_waves + first, chunk), :], pos_pieces)
            for part, values in enumerate(turns_cos_sin(turns)):
                where = pl.ds(chain * chain_rows + part * chain_waves + first, chunk)
                rounded = values.astype(jnp.bfloat16)
                phase[where, :] = rounded
                sums[where, :] = dot(rounded, queries)

    def cut(chain, stage):
        device, _, _, length = plans[chain][stage]
        place = chain * chain_rows + chain_rows - 2 * length
        return pltpu.make_async_remote_copy(
            src_ref=staged.at[pl.ds(place, length)],
            dst_ref=landed.at[pl.ds(place, length)],
            send_sem=cut_send.at[chain, stage],
            recv_sem=cut_recv.at[chain, stage],
            device_id=device,
            device_id_type=MESH,
        )

    def start_cut(chain, stage):
        _, _, send, length = plans[chain][stage]
        place = chain * chain_rows + chain_rows - 2 * length
        staged[pl.ds(place, length), :] = sums[
            pl.ds(pl.multiple_of(send, piece_rows), length), :
        ].astype(jnp.bfloat16)
        cut(chain, stage).start()

    def end_cut(chain, stage):
        cut(chain, stage).wait()
        _, keep, _, length = plans[chain][stage]
        place = chain * chain_rows + chain_rows - 2 * length
        where = pl.ds(pl.multiple_of(keep, piece_rows), length)
        sums[where, :] = sums[where, :] + landed[pl.ds(place, length), :].astype(jnp.float32)

    def join(chain, stage):
        device, keep, _, length = plans[chain][stage]
        where = pl.ds(pl.multiple_of(keep, piece_rows), length)
        return pltpu.make_async_remote_copy(
            src_ref=filtered.at[where],
            dst_ref=filtered.at[where],
            send_sem=join_send.at[chain, stage],
            recv_sem=join_recv.at[chain, stage],
            device_id=device,
            device_id_type=MESH,
        )

    def apply_gain(chain):
        _, mine, _, mine_rows = plans[chain][-1]
        scale = (atom_count * role_count * atoms_count) ** (-0.5) * ewald_scale
        channel = kgain[...] * scale
        where = pl.ds(pl.multiple_of(mine, piece_rows), mine_rows)
        first_wave = chain * chain_waves + (mine - chain * chain_rows) % chain_waves
        gain_rows = gain[pl.ds(pl.multiple_of(first_wave, piece_rows), mine_rows), :]
        for part in range(width // 128):
            lanes = pl.ds(part * 128, 128)
            filtered[where, lanes] = (
                sums[where, lanes] * gain_rows * channel[:, part * 128 : part * 128 + 128]
            ).astype(jnp.bfloat16)

    fill(0)
    start_cut(0, 0)
    for copy in halo:
        copy.wait()
    halo = [send_brick(2 + number, *move) for number, move in enumerate(along)]
    for chain in range(1, chains):
        fill(chain)
        start_cut(chain, 0)

    rbf_t[...] = flipped(w_rbf[...]).astype(jnp.bfloat16)
    filter_t[...] = flipped(w_filter[...]).astype(jnp.bfloat16)
    bias[...] = jnp.transpose(jnp.broadcast_to(b_rbf[...], (atom_count, width)))
    entry = neighbours[...]
    brick = entry // atom_count
    blocks[0] = brick.astype(jnp.float32)
    blocks[1] = (entry - brick * atom_count).astype(jnp.float32)
    image = images[...]
    first_part = jnp.where(image >= 9, 1, 0) + jnp.where(image >= 18, 1, 0)
    left = image - 9 * first_part
    second_part = jnp.where(left >= 3, 1, 0) + jnp.where(left >= 6, 1, 0)
    third_part = left - 3 * second_part
    for axis, part in enumerate((first_part, second_part, third_part)):
        offsets[axis] = (part - 1).astype(jnp.float32) - own[axis : axis + 1, :]
    messages[...] = jnp.zeros_like(messages)

    wave_part = waves[...]
    picks = jnp.where(
        lax.broadcasted_iota(jnp.int32, (waves.shape[1], 128), 0) < 3, 1.0, 0.0
    ).astype(jnp.bfloat16)
    squares = dot(wave_part * wave_part, picks)
    gain[...] = jnp.exp(squares * (-1.0 / damping)) / squares

    for chain in range(chains):
        end_cut(chain, 0)
        start_cut(chain, 1)

    @pl.loop(0, rows // chunk)
    def _(step):
        first = pl.multiple_of(step * chunk, chunk)
        phase_t[:, pl.ds(first, chunk)] = flipped(phase[pl.ds(first, chunk), :]).astype(
            jnp.bfloat16
        )

    lane_atoms = lax.broadcasted_iota(jnp.int32, (atom_count, atom_count), 0).astype(
        jnp.float32
    ).astype(jnp.bfloat16)
    centers = lax.broadcasted_iota(jnp.int32, (basis_count, atom_count), 0).astype(
        jnp.float32
    ) * (4.0 / (basis_count - 1))
    sharpness = (basis_count / 4.0) ** 2
    one, zero = jnp.ones((), jnp.bfloat16), jnp.zeros((), jnp.bfloat16)

    def gather(slot, target):
        brick_row = blocks[0, pl.ds(slot, 1), :]
        atom_row = blocks[1, pl.ds(slot, 1), :]
        chosen = []
        for number in range(9):
            wanted = jnp.where(brick_row == float(number), atom_row, -1.0).astype(jnp.bfloat16)
            chosen.append(jnp.where(lane_atoms == wanted, one, zero))
        bricks = jnp.concatenate([table[number] for number in range(9)], axis=1)
        target[...] = dot(bricks, jnp.concatenate(chosen, axis=0))

    def filter_slot(slot, source):
        square = jnp.full((1, atom_count), soft_sq, jnp.float32)
        for axis in range(3):
            near = (
                source[width + axis : width + axis + 1, :]
                + source[width + 3 + axis : width + 4 + axis, :]
                + source[width + 6 + axis : width + 7 + axis, :]
            )
            delta = near + offsets[axis, pl.ds(slot, 1), :]
            square += delta * delta
        away = jnp.sqrt(square) - centers
        basis = jnp.exp(-sharpness * (away * away)).astype(jnp.bfloat16)
        before = dot(rbf_t[...], basis) + bias[...]
        inner = (
            jnp.maximum(before, 0.0)
            + jnp.log(1.0 + jnp.exp(-jnp.abs(before)))
            - math.log(2.0)
        ).astype(jnp.bfloat16)
        messages[...] += dot(filter_t[...], inner) * source[0:width, :]

    def cut_event(chain, stage):
        end_cut(chain, stage)
        if stage + 1 < stages:
            start_cut(chain, stage + 1)
        else:
            apply_gain(chain)
            join(chain, stage).start()

    def join_event(chain, stage):
        join(chain, stage).wait()
        join(chain, stage - 1).start()

    events = [
        functools.partial(cut_event, chain, stage)
        for stage in range(1, stages)
        for chain in range(chains)
    ] + [
        functools.partial(join_event, chain, stage)
        for stage in reversed(range(1, stages))
        for chain in range(chains)
    ]

    for copy in halo:
        copy.wait()
    gather(0, wide_a)
    pairs = slot_count // 2

    @pl.loop(0, pairs)
    def _(pair):
        slot = pair * 2
        gather(slot + 1, wide_b)
        filter_slot(slot, wide_a)
        gather(lax.rem(slot + 2, slot_count), wide_a)
        filter_slot(slot + 1, wide_b)
        for number, event in enumerate(events):
            pl.when(pair == number * pairs // len(events))(event)

    short = jnp.transpose(messages[...]) * slot_count ** (-0.5)
    for chain in range(chains):
        join(chain, 0).wait()

    combined = (short + dot(phase_t[...], filtered[...])).astype(jnp.bfloat16)
    result[...] = (features[...].astype(jnp.float32) + dot(combined, w_out[...])).astype(
        jnp.bfloat16
    )


def local(
    role_count,
    atoms_count,
    features,
    positions,
    neighbours,
    images,
    wave,
    kgain,
    w_in,
    w_query,
    w_rbf,
    b_rbf,
    w_filter,
    w_out,
):
    own_rows = features[0, 0]
    atom_count, width = own_rows.shape
    wave_count = wave.shape[1]
    slot_count = neighbours.shape[2]
    rows = 2 * wave_count
    stages = (role_count * atoms_count).bit_length() - 1
    waves = jnp.transpose(
        jnp.pad(jnp.concatenate([wave] * 3, axis=0), ((0, piece_rows - 9), (0, 0)))
    ).astype(jnp.bfloat16)
    vmem = pl.BlockSpec(memory_space=pltpu.VMEM)
    full = width + coord_rows
    out = pl.pallas_call(
        functools.partial(block_kernel, role_count, atoms_count),
        out_shape=jax.ShapeDtypeStruct((atom_count, width), jnp.bfloat16),
        in_specs=[vmem] * 12,
        out_specs=vmem,
        scratch_shapes=[
            pltpu.VMEM((9, full, atom_count), jnp.bfloat16),
            pltpu.VMEM((piece_rows, atom_count), jnp.float32),
            pltpu.VMEM((rows, atom_count), jnp.bfloat16),
            pltpu.VMEM((atom_count, rows), jnp.bfloat16),
            pltpu.VMEM((rows, width), jnp.float32),
            pltpu.VMEM((rows, width), jnp.bfloat16),
            pltpu.VMEM((rows, width), jnp.bfloat16),
            pltpu.VMEM((rows, width), jnp.bfloat16),
            pltpu.VMEM((wave_count, 128), jnp.float32),
            pltpu.VMEM((3, slot_count, atom_count), jnp.float32),
            pltpu.VMEM((2, slot_count, atom_count), jnp.float32),
            pltpu.VMEM((full, atom_count), jnp.float32),
            pltpu.VMEM((full, atom_count), jnp.float32),
            pltpu.VMEM((width, atom_count), jnp.float32),
            pltpu.VMEM((width, w_rbf.shape[0]), jnp.bfloat16),
            pltpu.VMEM((width, width), jnp.bfloat16),
            pltpu.VMEM((width, atom_count), jnp.float32),
            pltpu.SemaphoreType.DMA((8,)),
            pltpu.SemaphoreType.DMA((8,)),
            pltpu.SemaphoreType.DMA((2, stages)),
            pltpu.SemaphoreType.DMA((2, stages)),
            pltpu.SemaphoreType.DMA((2, stages)),
            pltpu.SemaphoreType.DMA((2, stages)),
        ],
        compiler_params=pltpu.CompilerParams(
            collective_id=0, has_side_effects=True, vmem_limit_bytes=48 * 1024 * 1024
        ),
    )(
        own_rows,
        positions[0, 0],
        neighbours[0, 0],
        images[0, 0],
        waves,
        kgain[None, :],
        w_in,
        w_query,
        w_rbf,
        b_rbf[None, :],
        w_filter,
        w_out,
    )
    return out[None, None]


def solution(mesh):
    placed = P("role", "atoms", None, None)
    body = functools.partial(local, mesh.shape["role"], mesh.shape["atoms"])
    return jax.shard_map(
        body,
        mesh=mesh,
        in_specs=(placed,) * 4 + (P(),) * 8,
        out_specs=placed,
        check_vma=False,
    )
```

```python
import functools
import math

import jax
import jax.numpy as jnp
from jax import lax
from jax.experimental import pallas as pl
from jax.experimental.pallas import tpu as pltpu
from jax.sharding import PartitionSpec as P

soft_sq = 0.01
damping = 64.0
ewald_scale = 0.25
coord_rows = 16
piece_rows = 16
MESH = pl.DeviceIdType.MESH


def contract_first(left, right):
    return lax.dot_general(
        left, right, (((0,), (0,)), ((), ())), preferred_element_type=jnp.float32
    )


def dot(left, right):
    return jnp.dot(left, right, preferred_element_type=jnp.float32)


def flipped(array):
    return jnp.transpose(array.astype(jnp.float32))


def turns_cos_sin(turns):
    r = turns - jnp.floor(turns + 0.5)
    u = r * r
    sin_half = jnp.full_like(u, -(math.pi**11) / math.factorial(11))
    for power in (9, 7, 5, 3, 1):
        sign = 1.0 if power % 4 == 1 else -1.0
        sin_half = sin_half * u + sign * math.pi**power / math.factorial(power)
    sin_half = sin_half * r
    cos_half = jnp.full_like(u, math.pi**12 / math.factorial(12))
    for power in (10, 8, 6, 4, 2, 0):
        sign = 1.0 if power % 4 == 0 else -1.0
        cos_half = cos_half * u + sign * math.pi**power / math.factorial(power)
    return 1.0 - 2.0 * sin_half * sin_half, 2.0 * sin_half * cos_half


def exchange_plan(role_count, atoms_count, start, rows):
    role, atoms = lax.axis_index("role"), lax.axis_index("atoms")
    core = atoms % 2
    role_bits = role_count.bit_length() - 1
    atom_bits = atoms_count.bit_length() - 1
    partners = [(core, (role, atoms + 1 - 2 * core))]
    for stage in range(role_bits):
        if role_bits == 2:
            which = (stage + core) % 2
            low, high = role % 2, (role // 2) % 2
            bit = low + which * (high - low)
            partners.append((bit, (role + (1 - 2 * bit) * (1 + which), atoms)))
        else:
            bit = (role // 2**stage) % 2
            partners.append((bit, (role + (1 - 2 * bit) * 2**stage, atoms)))
    for stage in range(1, atom_bits):
        bit = (atoms // 2**stage) % 2
        partners.append((bit, (role, atoms + (1 - 2 * bit) * 2**stage)))
    plan = []
    length = rows
    for bit, device in partners:
        length //= 2
        keep = start + bit * length
        send = start + (1 - bit) * length
        plan.append((device, keep, send, length))
        start = keep
    return plan


def block_kernel(
    role_count,
    atoms_count,
    features,
    positions,
    neighbours,
    images,
    wave,
    kgain,
    w_in,
    w_query,
    w_rbf,
    b_rbf,
    w_filter,
    w_out,
    result,
    waves,
    table,
    pieces,
    phase,
    phase_t,
    sums,
    staged,
    landed,
    filtered,
    gain,
    offsets,
    blocks,
    wide_a,
    wide_b,
    messages,
    rbf_t,
    filter_t,
    bias,
    halo_send,
    halo_recv,
    cut_send,
    cut_recv,
    join_send,
    join_recv,
):
    role, atoms = lax.axis_index("role"), lax.axis_index("atoms")
    atom_count, width = features.shape
    slot_count = neighbours.shape[0]
    wave_count = wave.shape[1]
    basis_count = w_rbf.shape[0]
    rows = 2 * wave_count
    chains = 2 if rows // (role_count * atoms_count) >= 2 * piece_rows else 1
    chain_rows = rows // chains
    chain_waves = wave_count // chains
    plans = [
        exchange_plan(role_count, atoms_count, chain * chain_rows, chain_rows)
        for chain in range(chains)
    ]
    plan = plans[0]
    stages = len(plan)
    beside, along = [], []
    for step in (-1, 1):
        device = ((role + step + role_count) % role_count, atoms)
        beside.append((device, 1, 1 - step, 1))
        device = (role, (atoms + step + atoms_count) % atoms_count)
        along.extend((device, p, p, 1 - step) for p in (1, 0, 2))

    barrier = pltpu.get_barrier_semaphore()
    greeted = [beside[0][0], beside[1][0], along[0][0], along[3][0]]
    for device in greeted:
        pl.semaphore_signal(barrier, inc=1, device_id=device, device_id_type=MESH)
    for device, _, _, _ in plan:
        pl.semaphore_signal(barrier, inc=1, device_id=device, device_id_type=MESH)

    own = positions[...]
    high = own.astype(jnp.bfloat16).astype(jnp.float32)
    rest = own - high
    middle = rest.astype(jnp.bfloat16).astype(jnp.float32)
    pieces[...] = jnp.zeros_like(pieces)
    pieces[0:3, :] = high
    pieces[3:6, :] = middle
    pieces[6:9, :] = rest - middle
    pos_pieces = pieces[...].astype(jnp.bfloat16)
    waves[...] = jnp.zeros_like(waves)
    for copy_number in range(3):
        waves[copy_number * 3 : copy_number * 3 + 3, :] = wave[...].astype(jnp.float32)
    hidden = dot(features[...], w_in[...]).astype(jnp.bfloat16)
    table[4, 0:width, :] = flipped(hidden).astype(jnp.bfloat16)
    table[4, width : width + coord_rows, :] = pos_pieces

    pl.semaphore_wait(barrier, len(greeted) + len(plan))

    def send_brick(number, device, p, to_p, to_q):
        copy = pltpu.make_async_remote_copy(
            src_ref=table.at[p * 3 + 1],
            dst_ref=table.at[to_p * 3 + to_q],
            send_sem=halo_send.at[number],
            recv_sem=halo_recv.at[number],
            device_id=device,
            device_id_type=MESH,
        )
        copy.start()
        return copy

    halo = [send_brick(number, *move) for number, move in enumerate(beside)]

    queries = dot(features[...], w_query[...]).astype(jnp.bfloat16)
    chunk = 256

    def wave_columns(first):
        return flipped(waves[:, pl.ds(pl.multiple_of(first, chunk), chunk)]).astype(jnp.bfloat16)

    def fill(chain):
        @pl.loop(0, chain_waves // chunk)
        def _(step):
            first = pl.multiple_of(step * chunk, chunk)
            turns = dot(wave_columns(chain * chain_waves + first), pos_pieces)
            for part, values in enumerate(turns_cos_sin(turns)):
                where = pl.ds(chain * chain_rows + part * chain_waves + first, chunk)
                rounded = values.astype(jnp.bfloat16)
                phase[where, :] = rounded
                sums[where, :] = dot(rounded, queries)

    def cut(chain, stage):
        device, _, _, length = plans[chain][stage]
        place = chain * chain_rows + chain_rows - 2 * length
        return pltpu.make_async_remote_copy(
            src_ref=staged.at[pl.ds(place, length)],
            dst_ref=landed.at[pl.ds(place, length)],
            send_sem=cut_send.at[chain, stage],
            recv_sem=cut_recv.at[chain, stage],
            device_id=device,
            device_id_type=MESH,
        )

    def start_cut(chain, stage):
        _, _, send, length = plans[chain][stage]
        place = chain * chain_rows + chain_rows - 2 * length
        staged[pl.ds(place, length), :] = sums[
            pl.ds(pl.multiple_of(send, piece_rows), length), :
        ].astype(jnp.bfloat16)
        cut(chain, stage).start()

    def end_cut(chain, stage):
        cut(chain, stage).wait()
        _, keep, _, length = plans[chain][stage]
        place = chain * chain_rows + chain_rows - 2 * length
        where = pl.ds(pl.multiple_of(keep, piece_rows), length)
        sums[where, :] = sums[where, :] + landed[pl.ds(place, length), :].astype(jnp.float32)

    def join(chain, stage):
        device, keep, _, length = plans[chain][stage]
        where = pl.ds(pl.multiple_of(keep, piece_rows), length)
        return pltpu.make_async_remote_copy(
            src_ref=filtered.at[where],
            dst_ref=filtered.at[where],
            send_sem=join_send.at[chain, stage],
            recv_sem=join_recv.at[chain, stage],
            device_id=device,
            device_id_type=MESH,
        )

    def apply_gain(chain):
        _, mine, _, mine_rows = plans[chain][-1]
        scale = (atom_count * role_count * atoms_count) ** (-0.5) * ewald_scale
        channel = kgain[...] * scale
        where = pl.ds(pl.multiple_of(mine, piece_rows), mine_rows)
        first_wave = chain * chain_waves + (mine - chain * chain_rows) % chain_waves
        gain_rows = gain[pl.ds(pl.multiple_of(first_wave, piece_rows), mine_rows), :]
        for part in range(width // 128):
            lanes = pl.ds(part * 128, 128)
            filtered[where, lanes] = (
                sums[where, lanes] * gain_rows * channel[:, part * 128 : part * 128 + 128]
            ).astype(jnp.bfloat16)

    fill(0)
    start_cut(0, 0)
    for copy in halo:
        copy.wait()
    halo = [send_brick(2 + number, *move) for number, move in enumerate(along)]
    for chain in range(1, chains):
        fill(chain)
        start_cut(chain, 0)

    rbf_t[...] = flipped(w_rbf[...]).astype(jnp.bfloat16)
    filter_t[...] = flipped(w_filter[...]).astype(jnp.bfloat16)
    bias[...] = jnp.transpose(jnp.broadcast_to(b_rbf[...], (atom_count, width)))
    entry = neighbours[...]
    brick = entry // atom_count
    blocks[0] = brick.astype(jnp.float32)
    blocks[1] = (entry - brick * atom_count).astype(jnp.float32)
    image = images[...]
    first_part = jnp.where(image >= 9, 1, 0) + jnp.where(image >= 18, 1, 0)
    left = image - 9 * first_part
    second_part = jnp.where(left >= 3, 1, 0) + jnp.where(left >= 6, 1, 0)
    third_part = left - 3 * second_part
    for axis, part in enumerate((first_part, second_part, third_part)):
        offsets[axis] = (part - 1).astype(jnp.float32) - own[axis : axis + 1, :]
    messages[...] = jnp.zeros_like(messages)

    picks = jnp.where(
        lax.broadcasted_iota(jnp.int32, (piece_rows, 128), 0) < 3, 1.0, 0.0
    ).astype(jnp.bfloat16)

    @pl.loop(0, wave_count // chunk)
    def _(step):
        first = pl.multiple_of(step * chunk, chunk)
        columns = wave_columns(first)
        squares = dot(columns * columns, picks)
        gain[pl.ds(first, chunk), :] = jnp.exp(squares * (-1.0 / damping)) / squares


    for chain in range(chains):
        end_cut(chain, 0)
        start_cut(chain, 1)

    def turn_phase(step):
        first = pl.multiple_of(step * chunk, chunk)
        phase_t[:, pl.ds(first, chunk)] = flipped(phase[pl.ds(first, chunk), :]).astype(
            jnp.bfloat16
        )

    lane_atoms = lax.broadcasted_iota(jnp.int32, (atom_count, atom_count), 0).astype(
        jnp.float32
    ).astype(jnp.bfloat16)
    centers = lax.broadcasted_iota(jnp.int32, (basis_count, atom_count), 0).astype(
        jnp.float32
    ) * (4.0 / (basis_count - 1))
    sharpness = (basis_count / 4.0) ** 2
    one, zero = jnp.ones((), jnp.bfloat16), jnp.zeros((), jnp.bfloat16)

    def gather(slot, target):
        brick_row = blocks[0, pl.ds(slot, 1), :]
        atom_row = blocks[1, pl.ds(slot, 1), :]
        chosen = []
        for number in range(9):
            wanted = jnp.where(brick_row == float(number), atom_row, -1.0).astype(jnp.bfloat16)
            chosen.append(jnp.where(lane_atoms == wanted, one, zero))
        bricks = jnp.concatenate([table[number] for number in range(9)], axis=1)
        target[...] = dot(bricks, jnp.concatenate(chosen, axis=0))

    def filter_slot(slot, source):
        square = jnp.full((1, atom_count), soft_sq, jnp.float32)
        for axis in range(3):
            near = (
                source[width + axis : width + axis + 1, :]
                + source[width + 3 + axis : width + 4 + axis, :]
                + source[width + 6 + axis : width + 7 + axis, :]
            )
            delta = near + offsets[axis, pl.ds(slot, 1), :]
            square += delta * delta
        away = jnp.sqrt(square) - centers
        basis = jnp.exp(-sharpness * (away * away)).astype(jnp.bfloat16)
        before = dot(rbf_t[...], basis) + bias[...]
        inner = (
            jnp.maximum(before, 0.0)
            + jnp.log(1.0 + jnp.exp(-jnp.abs(before)))
            - math.log(2.0)
        ).astype(jnp.bfloat16)
        messages[...] += dot(filter_t[...], inner) * source[0:width, :]

    def cut_event(chain, stage):
        end_cut(chain, stage)
        if stage + 1 < stages:
            start_cut(chain, stage + 1)
        else:
            apply_gain(chain)
            join(chain, stage).start()

    def join_event(chain, stage):
        join(chain, stage).wait()
        join(chain, stage - 1).start()

    events = [
        functools.partial(cut_event, chain, stage)
        for stage in range(1, stages)
        for chain in range(chains)
    ] + [
        functools.partial(join_event, chain, stage)
        for stage in reversed(range(1, stages))
        for chain in range(chains)
    ]

    early = chains
    for event in events[:early]:
        event()
    for copy in halo:
        copy.wait()
    gather(0, wide_a)
    pairs = slot_count // 2
    late = events[early:]
    turned = rows // chunk
    for step in range(pairs, turned):
        turn_phase(step)

    @pl.loop(0, pairs)
    def _(pair):
        slot = pair * 2
        gather(slot + 1, wide_b)
        filter_slot(slot, wide_a)
        gather(lax.rem(slot + 2, slot_count), wide_a)
        filter_slot(slot + 1, wide_b)
        if turned >= pairs:
            turn_phase(pair)
        else:
            pl.when(pair < turned)(functools.partial(turn_phase, pair))
        for number, event in enumerate(late):
            pl.when(pair == number * (pairs - 1) // len(late))(event)

    short = jnp.transpose(messages[...]) * slot_count ** (-0.5)
    for chain in range(chains):
        join(chain, 0).wait()

    combined = (short + dot(phase_t[...], filtered[...])).astype(jnp.bfloat16)
    result[...] = (features[...].astype(jnp.float32) + dot(combined, w_out[...])).astype(
        jnp.bfloat16
    )


def local(
    role_count,
    atoms_count,
    features,
    positions,
    neighbours,
    images,
    wave,
    kgain,
    w_in,
    w_query,
    w_rbf,
    b_rbf,
    w_filter,
    w_out,
):
    own_rows = features[0, 0]
    atom_count, width = own_rows.shape
    wave_count = wave.shape[1]
    slot_count = neighbours.shape[2]
    rows = 2 * wave_count
    stages = (role_count * atoms_count).bit_length() - 1
    vmem = pl.BlockSpec(memory_space=pltpu.VMEM)
    full = width + coord_rows
    out = pl.pallas_call(
        functools.partial(block_kernel, role_count, atoms_count),
        out_shape=jax.ShapeDtypeStruct((atom_count, width), jnp.bfloat16),
        in_specs=[vmem] * 12,
        out_specs=vmem,
        scratch_shapes=[
            pltpu.VMEM((piece_rows, wave_count), jnp.float32),
            pltpu.VMEM((9, full, atom_count), jnp.bfloat16),
            pltpu.VMEM((piece_rows, atom_count), jnp.float32),
            pltpu.VMEM((rows, atom_count), jnp.bfloat16),
            pltpu.VMEM((atom_count, rows), jnp.bfloat16),
            pltpu.VMEM((rows, width), jnp.float32),
            pltpu.VMEM((rows, width), jnp.bfloat16),
            pltpu.VMEM((rows, width), jnp.bfloat16),
            pltpu.VMEM((rows, width), jnp.bfloat16),
            pltpu.VMEM((wave_count, 128), jnp.float32),
            pltpu.VMEM((3, slot_count, atom_count), jnp.float32),
            pltpu.VMEM((2, slot_count, atom_count), jnp.float32),
            pltpu.VMEM((full, atom_count), jnp.float32),
            pltpu.VMEM((full, atom_count), jnp.float32),
            pltpu.VMEM((width, atom_count), jnp.float32),
            pltpu.VMEM((width, w_rbf.shape[0]), jnp.bfloat16),
            pltpu.VMEM((width, width), jnp.bfloat16),
            pltpu.VMEM((width, atom_count), jnp.float32),
            pltpu.SemaphoreType.DMA((8,)),
            pltpu.SemaphoreType.DMA((8,)),
            pltpu.SemaphoreType.DMA((2, stages)),
            pltpu.SemaphoreType.DMA((2, stages)),
            pltpu.SemaphoreType.DMA((2, stages)),
            pltpu.SemaphoreType.DMA((2, stages)),
        ],
        compiler_params=pltpu.CompilerParams(
            collective_id=0, has_side_effects=True, vmem_limit_bytes=48 * 1024 * 1024
        ),
    )(
        own_rows,
        positions[0, 0],
        neighbours[0, 0],
        images[0, 0],
        wave,
        kgain[None, :],
        w_in,
        w_query,
        w_rbf,
        b_rbf[None, :],
        w_filter,
        w_out,
    )
    return out[None, None]


def solution(mesh):
    placed = P("role", "atoms", None, None)
    body = functools.partial(local, mesh.shape["role"], mesh.shape["atoms"])
    return jax.shard_map(
        body,
        mesh=mesh,
        in_specs=(placed,) * 4 + (P(),) * 8,
        out_specs=placed,
        check_vma=False,
    )
```

```python
import functools
import math

import jax
import jax.numpy as jnp
from jax import lax
from jax.experimental import pallas as pl
from jax.experimental.pallas import tpu as pltpu
from jax.sharding import PartitionSpec as P

soft_sq = 0.01
damping = 64.0
ewald_scale = 0.25
coord_rows = 16
piece_rows = 16
MESH = pl.DeviceIdType.MESH


def contract_first(left, right):
    return lax.dot_general(
        left, right, (((0,), (0,)), ((), ())), preferred_element_type=jnp.float32
    )


def dot(left, right):
    return jnp.dot(left, right, preferred_element_type=jnp.float32)


def flipped(array):
    return jnp.transpose(array.astype(jnp.float32))


def turns_cos_sin(turns):
    r = turns - jnp.floor(turns + 0.5)
    u = r * r
    sin_half = jnp.full_like(u, -(math.pi**11) / math.factorial(11))
    for power in (9, 7, 5, 3, 1):
        sign = 1.0 if power % 4 == 1 else -1.0
        sin_half = sin_half * u + sign * math.pi**power / math.factorial(power)
    sin_half = sin_half * r
    cos_half = jnp.full_like(u, math.pi**12 / math.factorial(12))
    for power in (10, 8, 6, 4, 2, 0):
        sign = 1.0 if power % 4 == 0 else -1.0
        cos_half = cos_half * u + sign * math.pi**power / math.factorial(power)
    return 1.0 - 2.0 * sin_half * sin_half, 2.0 * sin_half * cos_half


def exchange_plan(role_count, atoms_count, start, rows):
    role, atoms = lax.axis_index("role"), lax.axis_index("atoms")
    core = atoms % 2
    role_bits = role_count.bit_length() - 1
    atom_bits = atoms_count.bit_length() - 1
    partners = [(core, (role, atoms + 1 - 2 * core))]
    for stage in range(role_bits):
        if role_bits == 2:
            which = (stage + core) % 2
            low, high = role % 2, (role // 2) % 2
            bit = low + which * (high - low)
            partners.append((bit, (role + (1 - 2 * bit) * (1 + which), atoms)))
        else:
            bit = (role // 2**stage) % 2
            partners.append((bit, (role + (1 - 2 * bit) * 2**stage, atoms)))
    for stage in range(1, atom_bits):
        bit = (atoms // 2**stage) % 2
        partners.append((bit, (role, atoms + (1 - 2 * bit) * 2**stage)))
    plan = []
    length = rows
    for bit, device in partners:
        length //= 2
        keep = start + bit * length
        send = start + (1 - bit) * length
        plan.append((device, keep, send, length))
        start = keep
    return plan


def block_kernel(
    role_count,
    atoms_count,
    features,
    positions,
    neighbours,
    images,
    waves,
    kgain,
    w_in,
    w_query,
    w_rbf,
    b_rbf,
    w_filter,
    w_out,
    result,
    table,
    pieces,
    phase,
    phase_t,
    sums,
    staged,
    landed,
    filtered,
    gain,
    offsets,
    blocks,
    wide_a,
    wide_b,
    messages,
    rbf_t,
    filter_t,
    bias,
    halo_send,
    halo_recv,
    cut_send,
    cut_recv,
    join_send,
    join_recv,
):
    role, atoms = lax.axis_index("role"), lax.axis_index("atoms")
    atom_count, width = features.shape
    slot_count = neighbours.shape[0]
    wave_count = waves.shape[0]
    basis_count = w_rbf.shape[0]
    rows = 2 * wave_count
    chains = 2 if rows // (role_count * atoms_count) >= 2 * piece_rows else 1
    chain_rows = rows // chains
    chain_waves = wave_count // chains
    plans = [
        exchange_plan(role_count, atoms_count, chain * chain_rows, chain_rows)
        for chain in range(chains)
    ]
    plan = plans[0]
    stages = len(plan)
    beside, along = [], []
    for step in (-1, 1):
        device = ((role + step + role_count) % role_count, atoms)
        beside.append((device, 1, 1 - step, 1))
        device = (role, (atoms + step + atoms_count) % atoms_count)
        along.extend((device, p, p, 1 - step) for p in (1, 0, 2))

    barrier = pltpu.get_barrier_semaphore()
    greeted = [beside[0][0], beside[1][0], along[0][0], along[3][0]]
    for device in greeted:
        pl.semaphore_signal(barrier, inc=1, device_id=device, device_id_type=MESH)
    for device, _, _, _ in plan:
        pl.semaphore_signal(barrier, inc=1, device_id=device, device_id_type=MESH)

    own = positions[...]
    high = own.astype(jnp.bfloat16).astype(jnp.float32)
    rest = own - high
    middle = rest.astype(jnp.bfloat16).astype(jnp.float32)
    pieces[...] = jnp.zeros_like(pieces)
    pieces[0:3, :] = high
    pieces[3:6, :] = middle
    pieces[6:9, :] = rest - middle
    pos_pieces = pieces[...].astype(jnp.bfloat16)
    hidden = dot(features[...], w_in[...]).astype(jnp.bfloat16)
    table[4, 0:width, :] = flipped(hidden).astype(jnp.bfloat16)
    table[4, width : width + coord_rows, :] = pos_pieces

    pl.semaphore_wait(barrier, len(greeted) + len(plan))

    def send_brick(number, device, p, to_p, to_q):
        copy = pltpu.make_async_remote_copy(
            src_ref=table.at[p * 3 + 1],
            dst_ref=table.at[to_p * 3 + to_q],
            send_sem=halo_send.at[number],
            recv_sem=halo_recv.at[number],
            device_id=device,
            device_id_type=MESH,
        )
        copy.start()
        return copy

    halo = [send_brick(number, *move) for number, move in enumerate(beside)]

    queries = dot(features[...], w_query[...]).astype(jnp.bfloat16)
    chunk = 256

    def fill(chain):
        @pl.loop(0, chain_waves // chunk)
        def _(step):
            first = pl.multiple_of(step * chunk, chunk)
            turns = dot(waves[pl.ds(chain * chain_waves + first, chunk), :], pos_pieces)
            for part, values in enumerate(turns_cos_sin(turns)):
                where = pl.ds(chain * chain_rows + part * chain_waves + first, chunk)
                rounded = values.astype(jnp.bfloat16)
                phase[where, :] = rounded
                sums[where, :] = dot(rounded, queries)

    def cut(chain, stage):
        device, _, _, length = plans[chain][stage]
        place = chain * chain_rows + chain_rows - 2 * length
        return pltpu.make_async_remote_copy(
            src_ref=staged.at[pl.ds(place, length)],
            dst_ref=landed.at[pl.ds(place, length)],
            send_sem=cut_send.at[chain, stage],
            recv_sem=cut_recv.at[chain, stage],
            device_id=device,
            device_id_type=MESH,
        )

    def start_cut(chain, stage):
        _, _, send, length = plans[chain][stage]
        place = chain * chain_rows + chain_rows - 2 * length
        staged[pl.ds(place, length), :] = sums[
            pl.ds(pl.multiple_of(send, piece_rows), length), :
        ].astype(jnp.bfloat16)
        cut(chain, stage).start()

    def end_cut(chain, stage):
        cut(chain, stage).wait()
        _, keep, _, length = plans[chain][stage]
        place = chain * chain_rows + chain_rows - 2 * length
        where = pl.ds(pl.multiple_of(keep, piece_rows), length)
        sums[where, :] = sums[where, :] + landed[pl.ds(place, length), :].astype(jnp.float32)

    def join(chain, stage):
        device, keep, _, length = plans[chain][stage]
        where = pl.ds(pl.multiple_of(keep, piece_rows), length)
        return pltpu.make_async_remote_copy(
            src_ref=filtered.at[where],
            dst_ref=filtered.at[where],
            send_sem=join_send.at[chain, stage],
            recv_sem=join_recv.at[chain, stage],
            device_id=device,
            device_id_type=MESH,
        )

    def apply_gain(chain):
        _, mine, _, mine_rows = plans[chain][-1]
        scale = (atom_count * role_count * atoms_count) ** (-0.5) * ewald_scale
        channel = kgain[...] * scale
        where = pl.ds(pl.multiple_of(mine, piece_rows), mine_rows)
        first_wave = chain * chain_waves + (mine - chain * chain_rows) % chain_waves
        gain_rows = gain[pl.ds(pl.multiple_of(first_wave, piece_rows), mine_rows), :]
        for part in range(width // 128):
            lanes = pl.ds(part * 128, 128)
            filtered[where, lanes] = (
                sums[where, lanes] * gain_rows * channel[:, part * 128 : part * 128 + 128]
            ).astype(jnp.bfloat16)

    fill(0)
    start_cut(0, 0)
    for copy in halo:
        copy.wait()
    halo = [send_brick(2 + number, *move) for number, move in enumerate(along)]
    for chain in range(1, chains):
        fill(chain)
        start_cut(chain, 0)

    rbf_t[...] = flipped(w_rbf[...]).astype(jnp.bfloat16)
    filter_t[...] = flipped(w_filter[...]).astype(jnp.bfloat16)
    bias[...] = jnp.transpose(jnp.broadcast_to(b_rbf[...], (atom_count, width)))
    entry = neighbours[...]
    brick = entry // atom_count
    blocks[0] = brick.astype(jnp.float32)
    blocks[1] = (entry - brick * atom_count).astype(jnp.float32)
    image = images[...]
    first_part = jnp.where(image >= 9, 1, 0) + jnp.where(image >= 18, 1, 0)
    left = image - 9 * first_part
    second_part = jnp.where(left >= 3, 1, 0) + jnp.where(left >= 6, 1, 0)
    third_part = left - 3 * second_part
    for axis, part in enumerate((first_part, second_part, third_part)):
        offsets[axis] = (part - 1).astype(jnp.float32) - own[axis : axis + 1, :]
    messages[...] = jnp.zeros_like(messages)

    wave_part = waves[...]
    picks = jnp.where(
        lax.broadcasted_iota(jnp.int32, (waves.shape[1], 128), 0) < 3, 1.0, 0.0
    ).astype(jnp.bfloat16)
    squares = dot(wave_part * wave_part, picks)
    gain[...] = jnp.exp(squares * (-1.0 / damping)) / squares

    for chain in range(chains):
        end_cut(chain, 0)
        start_cut(chain, 1)

    square_shape = (atom_count, atom_count)
    on_diagonal = lax.broadcasted_iota(jnp.int32, square_shape, 0) == lax.broadcasted_iota(
        jnp.int32, square_shape, 1
    )
    identity = jnp.where(on_diagonal, 1.0, 0.0).astype(jnp.bfloat16)

    @pl.loop(0, rows // chunk)
    def _(step):
        first = pl.multiple_of(step * chunk, chunk)
        phase_t[:, pl.ds(first, chunk)] = lax.dot_general(
            identity,
            phase[pl.ds(first, chunk), :],
            (((1,), (1,)), ((), ())),
            preferred_element_type=jnp.float32,
        ).astype(jnp.bfloat16)

    lane_atoms = lax.broadcasted_iota(jnp.int32, (atom_count, atom_count), 0).astype(
        jnp.float32
    ).astype(jnp.bfloat16)
    centers = lax.broadcasted_iota(jnp.int32, (basis_count, atom_count), 0).astype(
        jnp.float32
    ) * (4.0 / (basis_count - 1))
    sharpness = (basis_count / 4.0) ** 2
    one, zero = jnp.ones((), jnp.bfloat16), jnp.zeros((), jnp.bfloat16)

    def gather(slot, target):
        brick_row = blocks[0, pl.ds(slot, 1), :]
        atom_row = blocks[1, pl.ds(slot, 1), :]
        chosen = []
        for number in range(9):
            wanted = jnp.where(brick_row == float(number), atom_row, -1.0).astype(jnp.bfloat16)
            chosen.append(jnp.where(lane_atoms == wanted, one, zero))
        bricks = jnp.concatenate([table[number] for number in range(9)], axis=1)
        target[...] = dot(bricks, jnp.concatenate(chosen, axis=0))

    def filter_slot(slot, source):
        square = jnp.full((1, atom_count), soft_sq, jnp.float32)
        for axis in range(3):
            near = (
                source[width + axis : width + axis + 1, :]
                + source[width + 3 + axis : width + 4 + axis, :]
                + source[width + 6 + axis : width + 7 + axis, :]
            )
            delta = near + offsets[axis, pl.ds(slot, 1), :]
            square += delta * delta
        away = jnp.sqrt(square) - centers
        basis = jnp.exp(-sharpness * (away * away)).astype(jnp.bfloat16)
        before = dot(rbf_t[...], basis) + bias[...]
        inner = (
            jnp.maximum(before, 0.0)
            + jnp.log(1.0 + jnp.exp(-jnp.abs(before)))
            - math.log(2.0)
        ).astype(jnp.bfloat16)
        messages[...] += dot(filter_t[...], inner) * source[0:width, :]

    def cut_event(chain, stage):
        end_cut(chain, stage)
        if stage + 1 < stages:
            start_cut(chain, stage + 1)
        else:
            apply_gain(chain)
            join(chain, stage).start()

    def join_event(chain, stage):
        join(chain, stage).wait()
        join(chain, stage - 1).start()

    events = [
        functools.partial(cut_event, chain, stage)
        for stage in range(1, stages)
        for chain in range(chains)
    ] + [
        functools.partial(join_event, chain, stage)
        for stage in reversed(range(1, stages))
        for chain in range(chains)
    ]

    early = chains
    for event in events[:early]:
        event()
    for copy in halo:
        copy.wait()
    gather(0, wide_a)
    pairs = slot_count // 2
    late = events[early:]

    @pl.loop(0, pairs)
    def _(pair):
        slot = pair * 2
        gather(slot + 1, wide_b)
        filter_slot(slot, wide_a)
        gather(lax.rem(slot + 2, slot_count), wide_a)
        filter_slot(slot + 1, wide_b)
        for number, event in enumerate(late):
            pl.when(pair == number * (pairs - 1) // len(late))(event)

    short = jnp.transpose(messages[...]) * slot_count ** (-0.5)
    for chain in range(chains):
        join(chain, 0).wait()

    combined = (short + dot(phase_t[...], filtered[...])).astype(jnp.bfloat16)
    result[...] = (features[...].astype(jnp.float32) + dot(combined, w_out[...])).astype(
        jnp.bfloat16
    )


def local(
    role_count,
    atoms_count,
    features,
    positions,
    neighbours,
    images,
    wave,
    kgain,
    w_in,
    w_query,
    w_rbf,
    b_rbf,
    w_filter,
    w_out,
):
    own_rows = features[0, 0]
    atom_count, width = own_rows.shape
    wave_count = wave.shape[1]
    slot_count = neighbours.shape[2]
    rows = 2 * wave_count
    stages = (role_count * atoms_count).bit_length() - 1
    waves = jnp.transpose(
        jnp.pad(jnp.concatenate([wave] * 3, axis=0), ((0, piece_rows - 9), (0, 0)))
    ).astype(jnp.bfloat16)
    vmem = pl.BlockSpec(memory_space=pltpu.VMEM)
    full = width + coord_rows
    out = pl.pallas_call(
        functools.partial(block_kernel, role_count, atoms_count),
        out_shape=jax.ShapeDtypeStruct((atom_count, width), jnp.bfloat16),
        in_specs=[vmem] * 12,
        out_specs=vmem,
        scratch_shapes=[
            pltpu.VMEM((9, full, atom_count), jnp.bfloat16),
            pltpu.VMEM((piece_rows, atom_count), jnp.float32),
            pltpu.VMEM((rows, atom_count), jnp.bfloat16),
            pltpu.VMEM((atom_count, rows), jnp.bfloat16),
            pltpu.VMEM((rows, width), jnp.float32),
            pltpu.VMEM((rows, width), jnp.bfloat16),
            pltpu.VMEM((rows, width), jnp.bfloat16),
            pltpu.VMEM((rows, width), jnp.bfloat16),
            pltpu.VMEM((wave_count, 128), jnp.float32),
            pltpu.VMEM((3, slot_count, atom_count), jnp.float32),
            pltpu.VMEM((2, slot_count, atom_count), jnp.float32),
            pltpu.VMEM((full, atom_count), jnp.float32),
            pltpu.VMEM((full, atom_count), jnp.float32),
            pltpu.VMEM((width, atom_count), jnp.float32),
            pltpu.VMEM((width, w_rbf.shape[0]), jnp.bfloat16),
            pltpu.VMEM((width, width), jnp.bfloat16),
            pltpu.VMEM((width, atom_count), jnp.float32),
            pltpu.SemaphoreType.DMA((8,)),
            pltpu.SemaphoreType.DMA((8,)),
            pltpu.SemaphoreType.DMA((2, stages)),
            pltpu.SemaphoreType.DMA((2, stages)),
            pltpu.SemaphoreType.DMA((2, stages)),
            pltpu.SemaphoreType.DMA((2, stages)),
        ],
        compiler_params=pltpu.CompilerParams(
            collective_id=0, has_side_effects=True, vmem_limit_bytes=48 * 1024 * 1024
        ),
    )(
        own_rows,
        positions[0, 0],
        neighbours[0, 0],
        images[0, 0],
        waves,
        kgain[None, :],
        w_in,
        w_query,
        w_rbf,
        b_rbf[None, :],
        w_filter,
        w_out,
    )
    return out[None, None]


def solution(mesh):
    placed = P("role", "atoms", None, None)
    body = functools.partial(local, mesh.shape["role"], mesh.shape["atoms"])
    return jax.shard_map(
        body,
        mesh=mesh,
        in_specs=(placed,) * 4 + (P(),) * 8,
        out_specs=placed,
        check_vma=False,
    )
```

```python
import functools
import math

import jax
import jax.numpy as jnp
from jax import lax
from jax.experimental import pallas as pl
from jax.experimental.pallas import tpu as pltpu
from jax.sharding import PartitionSpec as P

soft_sq = 0.01
damping = 64.0
ewald_scale = 0.25
coord_rows = 16
piece_rows = 16
MESH = pl.DeviceIdType.MESH


def contract_first(left, right):
    return lax.dot_general(
        left, right, (((0,), (0,)), ((), ())), preferred_element_type=jnp.float32
    )


def dot(left, right):
    return jnp.dot(left, right, preferred_element_type=jnp.float32)


def flipped(array):
    return jnp.transpose(array.astype(jnp.float32))


def turns_cos_sin(turns):
    r = turns - jnp.floor(turns + 0.5)
    u = r * r
    sin_half = jnp.full_like(u, -(math.pi**11) / math.factorial(11))
    for power in (9, 7, 5, 3, 1):
        sign = 1.0 if power % 4 == 1 else -1.0
        sin_half = sin_half * u + sign * math.pi**power / math.factorial(power)
    sin_half = sin_half * r
    cos_half = jnp.full_like(u, math.pi**12 / math.factorial(12))
    for power in (10, 8, 6, 4, 2, 0):
        sign = 1.0 if power % 4 == 0 else -1.0
        cos_half = cos_half * u + sign * math.pi**power / math.factorial(power)
    return 1.0 - 2.0 * sin_half * sin_half, 2.0 * sin_half * cos_half


def exchange_plan(role_count, atoms_count, start, rows):
    role, atoms = lax.axis_index("role"), lax.axis_index("atoms")
    core = atoms % 2
    role_bits = role_count.bit_length() - 1
    atom_bits = atoms_count.bit_length() - 1
    partners = [(core, (role, atoms + 1 - 2 * core))]
    for stage in range(role_bits):
        if role_bits == 2:
            which = (stage + core) % 2
            low, high = role % 2, (role // 2) % 2
            bit = low + which * (high - low)
            partners.append((bit, (role + (1 - 2 * bit) * (1 + which), atoms)))
        else:
            bit = (role // 2**stage) % 2
            partners.append((bit, (role + (1 - 2 * bit) * 2**stage, atoms)))
    for stage in range(1, atom_bits):
        bit = (atoms // 2**stage) % 2
        partners.append((bit, (role, atoms + (1 - 2 * bit) * 2**stage)))
    plan = []
    length = rows
    for bit, device in partners:
        length //= 2
        keep = start + bit * length
        send = start + (1 - bit) * length
        plan.append((device, keep, send, length))
        start = keep
    return plan


def block_kernel(
    role_count,
    atoms_count,
    features,
    positions,
    neighbours,
    images,
    waves,
    kgain,
    w_in,
    w_query,
    w_rbf,
    b_rbf,
    w_filter,
    w_out,
    result,
    table,
    pieces,
    phase,
    phase_t,
    sums,
    staged,
    landed,
    filtered,
    gain,
    offsets,
    blocks,
    wide_a,
    wide_b,
    messages,
    rbf_t,
    filter_t,
    bias,
    halo_send,
    halo_recv,
    cut_send,
    cut_recv,
    join_send,
    join_recv,
):
    role, atoms = lax.axis_index("role"), lax.axis_index("atoms")
    atom_count, width = features.shape
    slot_count = neighbours.shape[0]
    wave_count = waves.shape[0]
    basis_count = w_rbf.shape[0]
    rows = 2 * wave_count
    chains = 2 if rows // (role_count * atoms_count) >= 2 * piece_rows else 1
    chain_rows = rows // chains
    chain_waves = wave_count // chains
    plans = [
        exchange_plan(role_count, atoms_count, chain * chain_rows, chain_rows)
        for chain in range(chains)
    ]
    plan = plans[0]
    stages = len(plan)
    beside, along = [], []
    for step in (-1, 1):
        device = ((role + step + role_count) % role_count, atoms)
        beside.append((device, 1, 1 - step, 1))
        device = (role, (atoms + step + atoms_count) % atoms_count)
        along.extend((device, p, p, 1 - step) for p in (1, 0, 2))

    barrier = pltpu.get_barrier_semaphore()
    greeted = [beside[0][0], beside[1][0], along[0][0], along[3][0]]
    for device in greeted:
        pl.semaphore_signal(barrier, inc=1, device_id=device, device_id_type=MESH)
    for device, _, _, _ in plan:
        pl.semaphore_signal(barrier, inc=1, device_id=device, device_id_type=MESH)

    own = positions[...]
    high = own.astype(jnp.bfloat16).astype(jnp.float32)
    rest = own - high
    middle = rest.astype(jnp.bfloat16).astype(jnp.float32)
    pieces[...] = jnp.zeros_like(pieces)
    pieces[0:3, :] = high
    pieces[3:6, :] = middle
    pieces[6:9, :] = rest - middle
    pos_pieces = pieces[...].astype(jnp.bfloat16)
    hidden = dot(features[...], w_in[...]).astype(jnp.bfloat16)
    table[4, 0:width, :] = flipped(hidden).astype(jnp.bfloat16)
    table[4, width : width + coord_rows, :] = pos_pieces

    pl.semaphore_wait(barrier, len(greeted) + len(plan))

    def send_brick(number, device, p, to_p, to_q):
        copy = pltpu.make_async_remote_copy(
            src_ref=table.at[p * 3 + 1],
            dst_ref=table.at[to_p * 3 + to_q],
            send_sem=halo_send.at[number],
            recv_sem=halo_recv.at[number],
            device_id=device,
            device_id_type=MESH,
        )
        copy.start()
        return copy

    halo = [send_brick(number, *move) for number, move in enumerate(beside)]

    queries = dot(features[...], w_query[...]).astype(jnp.bfloat16)
    chunk = 256

    def fill(chain):
        @pl.loop(0, chain_waves // chunk)
        def _(step):
            first = pl.multiple_of(step * chunk, chunk)
            turns = dot(waves[pl.ds(chain * chain_waves + first, chunk), :], pos_pieces)
            for part, values in enumerate(turns_cos_sin(turns)):
                where = pl.ds(chain * chain_rows + part * chain_waves + first, chunk)
                rounded = values.astype(jnp.bfloat16)
                phase[where, :] = rounded
                sums[where, :] = dot(rounded, queries)

    def cut(chain, stage):
        device, _, _, length = plans[chain][stage]
        place = chain * chain_rows + chain_rows - 2 * length
        return pltpu.make_async_remote_copy(
            src_ref=staged.at[pl.ds(place, length)],
            dst_ref=landed.at[pl.ds(place, length)],
            send_sem=cut_send.at[chain, stage],
            recv_sem=cut_recv.at[chain, stage],
            device_id=device,
            device_id_type=MESH,
        )

    def start_cut(chain, stage):
        _, _, send, length = plans[chain][stage]
        place = chain * chain_rows + chain_rows - 2 * length
        staged[pl.ds(place, length), :] = sums[
            pl.ds(pl.multiple_of(send, piece_rows), length), :
        ].astype(jnp.bfloat16)
        cut(chain, stage).start()

    def end_cut(chain, stage):
        cut(chain, stage).wait()
        _, keep, _, length = plans[chain][stage]
        place = chain * chain_rows + chain_rows - 2 * length
        where = pl.ds(pl.multiple_of(keep, piece_rows), length)
        sums[where, :] = sums[where, :] + landed[pl.ds(place, length), :].astype(jnp.float32)

    def join(chain, stage):
        device, keep, _, length = plans[chain][stage]
        where = pl.ds(pl.multiple_of(keep, piece_rows), length)
        return pltpu.make_async_remote_copy(
            src_ref=filtered.at[where],
            dst_ref=filtered.at[where],
            send_sem=join_send.at[chain, stage],
            recv_sem=join_recv.at[chain, stage],
            device_id=device,
            device_id_type=MESH,
        )

    def apply_gain(chain):
        _, mine, _, mine_rows = plans[chain][-1]
        scale = (atom_count * role_count * atoms_count) ** (-0.5) * ewald_scale
        channel = kgain[...] * scale
        where = pl.ds(pl.multiple_of(mine, piece_rows), mine_rows)
        first_wave = chain * chain_waves + (mine - chain * chain_rows) % chain_waves
        gain_rows = gain[pl.ds(pl.multiple_of(first_wave, piece_rows), mine_rows), :]
        for part in range(width // 128):
            lanes = pl.ds(part * 128, 128)
            filtered[where, lanes] = (
                sums[where, lanes] * gain_rows * channel[:, part * 128 : part * 128 + 128]
            ).astype(jnp.bfloat16)

    fill(0)
    start_cut(0, 0)
    for copy in halo:
        copy.wait()
    halo = [send_brick(2 + number, *move) for number, move in enumerate(along)]
    for chain in range(1, chains):
        fill(chain)
        start_cut(chain, 0)

    rbf_t[...] = flipped(w_rbf[...]).astype(jnp.bfloat16)
    filter_t[...] = flipped(w_filter[...]).astype(jnp.bfloat16)
    bias[...] = jnp.transpose(jnp.broadcast_to(b_rbf[...], (atom_count, width)))
    entry = neighbours[...]
    brick = entry // atom_count
    blocks[0] = brick.astype(jnp.float32)
    blocks[1] = (entry - brick * atom_count).astype(jnp.float32)
    image = images[...]
    first_part = jnp.where(image >= 9, 1, 0) + jnp.where(image >= 18, 1, 0)
    left = image - 9 * first_part
    second_part = jnp.where(left >= 3, 1, 0) + jnp.where(left >= 6, 1, 0)
    third_part = left - 3 * second_part
    for axis, part in enumerate((first_part, second_part, third_part)):
        offsets[axis] = (part - 1).astype(jnp.float32) - own[axis : axis + 1, :]
    messages[...] = jnp.zeros_like(messages)

    wave_part = waves[...]
    picks = jnp.where(
        lax.broadcasted_iota(jnp.int32, (waves.shape[1], 128), 0) < 3, 1.0, 0.0
    ).astype(jnp.bfloat16)
    squares = dot(wave_part * wave_part, picks)
    gain[...] = jnp.exp(squares * (-1.0 / damping)) / squares

    for chain in range(chains):
        end_cut(chain, 0)
        start_cut(chain, 1)

    square_shape = (atom_count, atom_count)
    on_diagonal = lax.broadcasted_iota(jnp.int32, square_shape, 0) == lax.broadcasted_iota(
        jnp.int32, square_shape, 1
    )
    identity = jnp.where(on_diagonal, 1.0, 0.0).astype(jnp.bfloat16)

    @pl.loop(0, rows // chunk)
    def _(step):
        first = pl.multiple_of(step * chunk, chunk)
        phase_t[:, pl.ds(first, chunk)] = lax.dot_general(
            identity,
            phase[pl.ds(first, chunk), :],
            (((1,), (1,)), ((), ())),
            preferred_element_type=jnp.float32,
        ).astype(jnp.bfloat16)

    lane_atoms = lax.broadcasted_iota(jnp.int32, (atom_count, atom_count), 0).astype(
        jnp.float32
    ).astype(jnp.bfloat16)
    centers = lax.broadcasted_iota(jnp.int32, (basis_count, atom_count), 0).astype(
        jnp.float32
    ) * (4.0 / (basis_count - 1))
    sharpness = (basis_count / 4.0) ** 2
    one, zero = jnp.ones((), jnp.bfloat16), jnp.zeros((), jnp.bfloat16)

    def gather(slot, target):
        brick_row = blocks[0, pl.ds(slot, 1), :]
        atom_row = blocks[1, pl.ds(slot, 1), :]
        chosen = []
        for number in range(9):
            wanted = jnp.where(brick_row == float(number), atom_row, -1.0).astype(jnp.bfloat16)
            chosen.append(jnp.where(lane_atoms == wanted, one, zero))
        bricks = jnp.concatenate([table[number] for number in range(9)], axis=1)
        target[...] = dot(bricks, jnp.concatenate(chosen, axis=0))

    def filter_slot(slot, source):
        square = jnp.full((1, atom_count), soft_sq, jnp.float32)
        for axis in range(3):
            near = (
                source[width + axis : width + axis + 1, :]
                + source[width + 3 + axis : width + 4 + axis, :]
                + source[width + 6 + axis : width + 7 + axis, :]
            )
            delta = near + offsets[axis, pl.ds(slot, 1), :]
            square += delta * delta
        away = jnp.sqrt(square) - centers
        basis = jnp.exp(-sharpness * (away * away)).astype(jnp.bfloat16)
        before = dot(rbf_t[...], basis) + bias[...]
        inner = (
            jnp.maximum(before, 0.0)
            + jnp.log(1.0 + jnp.exp(-jnp.abs(before)))
            - math.log(2.0)
        ).astype(jnp.bfloat16)
        messages[...] += dot(filter_t[...], inner) * source[0:width, :]

    def cut_event(chain, stage):
        end_cut(chain, stage)
        if stage + 1 < stages:
            start_cut(chain, stage + 1)
        else:
            apply_gain(chain)
            join(chain, stage).start()

    def join_event(chain, stage):
        join(chain, stage).wait()
        join(chain, stage - 1).start()

    events = [
        functools.partial(cut_event, chain, stage)
        for stage in range(1, stages)
        for chain in range(chains)
    ] + [
        functools.partial(join_event, chain, stage)
        for stage in reversed(range(1, stages))
        for chain in range(chains)
    ]

    early = 0
    for event in events[:early]:
        event()
    for copy in halo:
        copy.wait()
    gather(0, wide_a)
    pairs = slot_count // 2
    late = events[early:]

    @pl.loop(0, pairs)
    def _(pair):
        slot = pair * 2
        gather(slot + 1, wide_b)
        filter_slot(slot, wide_a)
        gather(lax.rem(slot + 2, slot_count), wide_a)
        filter_slot(slot + 1, wide_b)
        for number, event in enumerate(late):
            pl.when(pair == number * pairs // len(late))(event)

    short = jnp.transpose(messages[...]) * slot_count ** (-0.5)
    for chain in range(chains):
        join(chain, 0).wait()

    combined = (short + dot(phase_t[...], filtered[...])).astype(jnp.bfloat16)
    result[...] = (features[...].astype(jnp.float32) + dot(combined, w_out[...])).astype(
        jnp.bfloat16
    )


def local(
    role_count,
    atoms_count,
    features,
    positions,
    neighbours,
    images,
    wave,
    kgain,
    w_in,
    w_query,
    w_rbf,
    b_rbf,
    w_filter,
    w_out,
):
    own_rows = features[0, 0]
    atom_count, width = own_rows.shape
    wave_count = wave.shape[1]
    slot_count = neighbours.shape[2]
    rows = 2 * wave_count
    stages = (role_count * atoms_count).bit_length() - 1
    waves = jnp.transpose(
        jnp.pad(jnp.concatenate([wave] * 3, axis=0), ((0, piece_rows - 9), (0, 0)))
    ).astype(jnp.bfloat16)
    vmem = pl.BlockSpec(memory_space=pltpu.VMEM)
    full = width + coord_rows
    out = pl.pallas_call(
        functools.partial(block_kernel, role_count, atoms_count),
        out_shape=jax.ShapeDtypeStruct((atom_count, width), jnp.bfloat16),
        in_specs=[vmem] * 12,
        out_specs=vmem,
        scratch_shapes=[
            pltpu.VMEM((9, full, atom_count), jnp.bfloat16),
            pltpu.VMEM((piece_rows, atom_count), jnp.float32),
            pltpu.VMEM((rows, atom_count), jnp.bfloat16),
            pltpu.VMEM((atom_count, rows), jnp.bfloat16),
            pltpu.VMEM((rows, width), jnp.float32),
            pltpu.VMEM((rows, width), jnp.bfloat16),
            pltpu.VMEM((rows, width), jnp.bfloat16),
            pltpu.VMEM((rows, width), jnp.bfloat16),
            pltpu.VMEM((wave_count, 128), jnp.float32),
            pltpu.VMEM((3, slot_count, atom_count), jnp.float32),
            pltpu.VMEM((2, slot_count, atom_count), jnp.float32),
            pltpu.VMEM((full, atom_count), jnp.float32),
            pltpu.VMEM((full, atom_count), jnp.float32),
            pltpu.VMEM((width, atom_count), jnp.float32),
            pltpu.VMEM((width, w_rbf.shape[0]), jnp.bfloat16),
            pltpu.VMEM((width, width), jnp.bfloat16),
            pltpu.VMEM((width, atom_count), jnp.float32),
            pltpu.SemaphoreType.DMA((8,)),
            pltpu.SemaphoreType.DMA((8,)),
            pltpu.SemaphoreType.DMA((2, stages)),
            pltpu.SemaphoreType.DMA((2, stages)),
            pltpu.SemaphoreType.DMA((2, stages)),
            pltpu.SemaphoreType.DMA((2, stages)),
        ],
        compiler_params=pltpu.CompilerParams(
            collective_id=0, has_side_effects=True, vmem_limit_bytes=48 * 1024 * 1024
        ),
    )(
        own_rows,
        positions[0, 0],
        neighbours[0, 0],
        images[0, 0],
        waves,
        kgain[None, :],
        w_in,
        w_query,
        w_rbf,
        b_rbf[None, :],
        w_filter,
        w_out,
    )
    return out[None, None]


def solution(mesh):
    placed = P("role", "atoms", None, None)
    body = functools.partial(local, mesh.shape["role"], mesh.shape["atoms"])
    return jax.shard_map(
        body,
        mesh=mesh,
        in_specs=(placed,) * 4 + (P(),) * 8,
        out_specs=placed,
        check_vma=False,
    )
```
